768 devices in a mesh: lat: 24 (over z_lo, y), lon: 32 (over z_hi, x, core).
Axes of the slice: x: 4, y: 8, z: 12 (z_hi: 4, z_lo: 3; z = z_hi * 3 + z_lo), core: 2. Of those that a mesh axis runs over, the one named last changes fastest.
Arguments:
- latent_field: bfloat16 [640, 192, 384], P(None, 'lat', 'lon'), may hold values from -6 to 6
- spectral_filter: float32 [640, 192], P('lon'), may hold values from -5 to 5
- conv_weight: float32 [9, 640], replicated, may hold values from -2 to 2
- norm_gain: float32 [640], replicated, may hold values from 0.1 to 1.9
- weight_in: bfloat16 [640, 1280], replicated, may hold values from -0.25 to 0.25
- weight_out: bfloat16 [1280, 640], replicated, may hold values from -0.15625 to 0.15625
Outputs:
- updated: bfloat16 [640, 192, 384], P(None, 'lat', 'lon')
The draws below stay inside these ranges and needn't reach their ends.
All inputs are finite; a program needn't handle non-finite values.
Results may differ from the reference program's by a relative error of at most 0.01.
Values may be sent and summed in bfloat16 or wider, within the bound.
No kernel may reach another device: no remote copies, remote signals or barrier semaphores. Data moves between devices by JAX's collectives and lax.ppermute only.
A program may use at most 128 MiB of HBM per device.

```python
import math
import jax
import jax.numpy as jnp
from jax import lax

C = 640
HID = 1280
LAT_DEV = 8
NLAT = 192
NLON = 384
N_LAT = 24
N_LON = 32


def steps_of(key, dims, cuts, least, largest):
    gain, own = 1.0, jax.random.fold_in(key, 6)
    for axis_at, parts in cuts:
        steps = jnp.exp(jax.random.uniform(jax.random.fold_in(own, axis_at), (parts,), jnp.float32, least / len(cuts), largest / len(cuts)))
        gain = gain * jnp.repeat(steps, dims[axis_at] // parts).reshape([-1 if axis == axis_at else 1 for axis in range(len(dims))])
    return gain


def scatter_about(own_key, dims, scale, bound, pieces=(), kind=jnp.bfloat16):
    drawn = jax.random.normal(own_key, dims, jnp.float32) * scale
    if len(pieces) > 0:
        drawn = steps_of(own_key, dims, pieces, -0.22, 0.18) * drawn
    return jnp.clip(drawn, min=-bound, max=bound).astype(kind)


def setup_inputs(seed: int = 0) -> dict:
    keys = jax.random.split(jax.random.key(seed), 7)
    return {
        "latent_field": scatter_about(keys[0], (C, NLAT, NLON), 1.0, 6.0, ((1, 24), (2, 32))),
        "spectral_filter": scatter_about(keys[1], (C, NLAT), 1.0, 5.0, ((0, 32),), jnp.float32),
        "conv_weight": scatter_about(keys[2], (9, C), 9 ** -0.5, 2.0, (), jnp.float32),
        "norm_gain": jnp.clip(1.0 + 0.18 * jax.random.normal(keys[3], (C,), jnp.float32), 0.1, 1.9),
        "weight_in": scatter_about(keys[4], (C, HID), C ** -0.5, 0.25),
        "weight_out": scatter_about(keys[5], (HID, C), HID ** -0.5, 0.15625),
    }


highest = lax.Precision.HIGHEST
epsilon_norm = 1e-06

def quadrature(lat_count):
    colatitude = (jnp.arange(lat_count, dtype=jnp.float32) + 0.5) * (math.pi / lat_count)
    return jnp.sin(colatitude) * (math.pi / lat_count)

def fourier_tables(lon_count, mode_count):
    wave_index = jnp.arange(mode_count, dtype=jnp.int32)[:, None] * jnp.arange(lon_count, dtype=jnp.int32)[None, :]
    phase_angle = (wave_index % lon_count).astype(jnp.float32) * (2.0 * math.pi / lon_count)
    cosine = jnp.cos(phase_angle)
    sine_table = jnp.sin(phase_angle)
    angle_step = 2.0 * math.pi / lon_count
    forward = jnp.concatenate([angle_step * cosine, -angle_step * sine_table], axis=0)
    weight = jnp.where(jnp.arange(mode_count, dtype=jnp.int32) == 0, 1.0, 2.0).astype(jnp.float32)[:, None]
    inverse = jnp.concatenate([weight * cosine, -weight * sine_table], axis=0)
    return (forward, inverse)

def legendre_rows(order_ids, lat_count):
    colatitude = (jnp.arange(lat_count, dtype=jnp.float32) + 0.5) * (math.pi / lat_count)
    cosine = jnp.cos(colatitude)
    sine_col = jnp.sin(colatitude)
    order_f = order_ids.astype(jnp.float32)
    factor_index = jnp.arange(1, lat_count, dtype=jnp.float32)
    ratio_log = jnp.log((2.0 * factor_index - 1.0) / (2.0 * factor_index))
    included = (factor_index[None, :] <= order_f[:, None]).astype(jnp.float32)
    log_factor = lax.optimization_barrier(jnp.sum(included * ratio_log[None, :], axis=1))
    start_log = 0.5 * jnp.log((2.0 * order_f + 1.0) / (4.0 * math.pi)) + 0.5 * log_factor
    start_log = start_log[:, None] + order_f[:, None] * jnp.log(sine_col)[None, :]
    blank_rows = jnp.zeros((order_ids.shape[0], lat_count), jnp.float32)
    order_col = order_f[:, None]

    def advance(state_carry, degree):
        before, current, scale_log = state_carry
        degree_f = degree.astype(jnp.float32)
        alpha_term = jnp.sqrt((4.0 * degree_f * degree_f - 1.0) / jnp.maximum(degree_f * degree_f - order_col * order_col, 1.0))
        beta_term = jnp.sqrt(jnp.maximum((degree_f - 1.0) ** 2 - order_col * order_col, 0.0) / jnp.maximum(4.0 * (degree_f - 1.0) ** 2 - 1.0, 1.0))
        stepped = alpha_term * (cosine[None, :] * current - beta_term * before)
        at_start = order_ids[:, None] == degree
        past_start = order_ids[:, None] < degree
        fresh_value = jnp.where(at_start, 1.0, jnp.where(past_start, stepped, 0.0))
        fresh_log = jnp.where(at_start, start_log, scale_log)
        entry_value = fresh_value * jnp.exp(fresh_log)
        rescale = jnp.where(past_start | at_start, jnp.maximum(jnp.abs(fresh_value), jnp.abs(current)), 1.0)
        return ((current / rescale, fresh_value / rescale, fresh_log + jnp.log(rescale)), entry_value)
    degrees = jnp.arange(lat_count, dtype=jnp.int32)
    unused, legendre = lax.scan(advance, (blank_rows, blank_rows, blank_rows), degrees, unroll=16)
    return legendre

def filter_modes(banded, legendre, filter_block, quad_weights):
    coefficients = jnp.einsum('lmj,pmcj->pmcl', legendre, banded * quad_weights[None, None, None, :], precision=highest)
    coefficients = coefficients * filter_block[None, None, :, :]
    return jnp.einsum('lmj,pmcl->pmcj', legendre, coefficients, precision=highest)

def wrap_columns(extended):
    return jnp.concatenate([extended[:, :, -1:], extended, extended[:, :, :1]], axis=2)

def depthwise_core(extended, kernel, lat_rows, lon_cols):
    accumulated = jnp.zeros((extended.shape[0], lat_rows, lon_cols), jnp.float32)
    for row_shift in range(3):
        for col_shift in range(3):
            piece = extended[:, row_shift:row_shift + lat_rows, col_shift:col_shift + lon_cols].astype(jnp.float32)
            accumulated = accumulated + kernel[3 * row_shift + col_shift][:, None, None] * piece
    return accumulated.astype(jnp.bfloat16)

def channel_mlp(summed_low, norm_gain, weight_in, weight_out):
    summed = summed_low.astype(jnp.float32)
    scale_inv = lax.rsqrt(lax.optimization_barrier(jnp.mean(summed * summed, axis=0, keepdims=True)) + epsilon_norm)
    normed = (summed * scale_inv * norm_gain[:, None]).astype(jnp.bfloat16)
    hidden = lax.dot_general(weight_in, normed, (((0,), (0,)), ((), ())), preferred_element_type=jnp.float32)
    hidden = jax.nn.gelu(hidden, approximate=False).astype(jnp.bfloat16)
    result = summed + lax.dot_general(weight_out, hidden, (((0,), (0,)), ((), ())), preferred_element_type=jnp.float32)
    return result.astype(jnp.bfloat16)

def row_blocks(array):
    return jnp.transpose(array.reshape(C, N_LAT, LAT_DEV * NLON), (1, 0, 2))

def reference(latent_field, spectral_filter, conv_weight, norm_gain, weight_in, weight_out):
    chan_block = C // N_LON
    forward, inverse = fourier_tables(NLON, NLAT)
    legendre = legendre_rows(jnp.arange(NLAT, dtype=jnp.int32), NLAT)
    quad_weights = quadrature(NLAT)
    field_blocks = latent_field.reshape(N_LON, chan_block, NLAT, NLON)
    filter_blocks = spectral_filter.reshape(N_LON, chan_block, NLAT)
    kernel_blocks = jnp.transpose(conv_weight.reshape(9, N_LON, chan_block), (1, 0, 2))

    def branch_pair(inputs):
        field_block, filter_block, kernel_block = inputs
        flattened = field_block.astype(jnp.float32).reshape(chan_block * NLAT, NLON)
        spectrum = lax.dot_general(forward, flattened, (((1,), (1,)), ((), ())), precision=highest)
        spectrum = spectrum.reshape(2, NLAT, chan_block, NLAT)
        synthesized = filter_modes(spectrum, legendre, filter_block, quad_weights)
        regridded = lax.dot_general(synthesized.reshape(2 * NLAT, chan_block * NLAT), inverse, (((0,), (0,)), ((), ())), precision=highest)
        spectral = regridded.reshape(chan_block, NLAT, NLON).astype(jnp.bfloat16)
        extended = jnp.pad(field_block, ((0, 0), (1, 1), (0, 0)))
        local_mix = depthwise_core(wrap_columns(extended), kernel_block, NLAT, NLON)
        return (spectral, local_mix)
    spectral, local_mix = lax.map(branch_pair, (field_blocks, filter_blocks, kernel_blocks))
    spectral = spectral.reshape(C, NLAT, NLON)
    local_mix = local_mix.reshape(C, NLAT, NLON)

    def mix_band(inputs):
        field_band, spectral_band, conv_band = inputs
        summed = field_band.astype(jnp.float32) + spectral_band.astype(jnp.float32) + conv_band.astype(jnp.float32)
        return channel_mlp(summed.astype(jnp.bfloat16), norm_gain, weight_in, weight_out)
    bands = lax.map(mix_band, (row_blocks(latent_field), row_blocks(spectral), row_blocks(local_mix)))
    return jnp.transpose(bands, (1, 0, 2)).reshape(C, NLAT, NLON)
```

```python
import functools
import math

import jax
import jax.numpy as jnp
from jax import lax
from jax.experimental import pallas as pl
from jax.experimental.pallas import tpu as pltpu
from jax.sharding import PartitionSpec as P

LON, LAT, COLS, ROWS, CHAN = 32, 24, 12, 8, 20
NLON, NLAT = LON * COLS, LAT * ROWS
PAIRS = COLS // 2
BF, F32 = jnp.bfloat16, jnp.float32
EPS = 1e-06


def lanes_of(shape):
    return lax.broadcasted_iota(jnp.int32, shape, 1)


def inside(shape, start, width):
    lane = lanes_of(shape)
    return (lane >= start) & (lane < start + width)


def turn(x, shift):
    shift %= 128
    return x if shift == 0 else pltpu.roll(x, shift, 1)


def call(body, outs, *args, scratch=(), name, mib=24, flops=0, in_specs=None):
    if in_specs is None:
        in_specs = [pl.BlockSpec(memory_space=pltpu.VMEM)] * len(args)
    single = isinstance(outs, tuple)
    result = pl.pallas_call(
        body,
        out_shape=[jax.ShapeDtypeStruct(*o) for o in ([outs] if single else outs)],
        in_specs=in_specs,
        out_specs=[pl.BlockSpec(memory_space=pltpu.VMEM)] * (1 if single else len(outs)),
        scratch_shapes=list(scratch),
        compiler_params=pltpu.CompilerParams(vmem_limit_bytes=mib * 2**20),
        cost_estimate=pl.CostEstimate(flops=flops, bytes_accessed=1_000_000, transcendentals=0),
        name=name,
    )(*args)
    return result[0] if single else result


def pack_body(x_ref, send_ref):
    shape = (16, 128)
    for d in range(LON):
        tile, off = divmod(CHAN * d, 128)
        total = jnp.zeros(shape, F32)
        for q in range(PAIRS):
            at = slice(16 * q, 16 * q + 16)
            piece = x_ref[at, 128 * tile : 128 * tile + 128].astype(F32)
            if off + CHAN > 128:
                after = x_ref[at, 128 * tile + 128 : 128 * tile + 256].astype(F32)
                piece = jnp.where(lanes_of(shape) >= off, piece, after)
            total = jnp.where(inside(shape, CHAN * q, CHAN), turn(piece, CHAN * q - off), total)
        send_ref[d] = total.astype(BF)


def wave(order, part, column):
    v = (order * column + part * (NLON // 4)).astype(F32)
    index = v - NLON * jnp.floor(v * (1.0 / NLON))
    x = (NLON // 4 - jnp.abs(index - NLON // 2)) * (2.0 * math.pi / NLON)
    y = x * x
    s = 1.0 / 6227020800.0
    for term in (-1.0 / 39916800.0, 1.0 / 362880.0, -1.0 / 5040.0, 1.0 / 120.0, -1.0 / 6.0, 1.0):
        s = s * y + term
    return -(s * x)


def mode_of(n):
    return ((n >> 4) << 3) + (n & 7), (n >> 3) & 1


def column_of(k):
    return COLS * (k & 31) + (k >> 5)


def halves(x):
    high = x.astype(BF)
    return high, (x - high.astype(F32)).astype(BF)


def fourier_body(fhi_ref, flo_ref, ihi_ref, ilo_ref):
    shape = (16, NLON)
    lane = lanes_of(shape)

    def block(b, unused):
        row = lax.broadcasted_iota(jnp.int32, shape, 0) + 16 * b
        at = pl.ds(pl.multiple_of(16 * b, 16), 16)
        order, part = mode_of(row)
        table = wave(order, part, column_of(lane)) * (2.0 * math.pi / NLON)
        fhi_ref[at, :], flo_ref[at, :] = halves(table)
        order, part = mode_of(lane)
        table = wave(order, part, column_of(row)) * jnp.where(order == 0, 1.0, 2.0)
        ihi_ref[at, :], ilo_ref[at, :] = halves(table)
        return unused

    lax.fori_loop(0, NLON // 16, block, 0)


def legendre_body(band_ref, pw_ref, pt_ref, table):
    shape = (8, 256)
    lane = lanes_of(shape)
    order_i = lax.broadcasted_iota(jnp.int32, shape, 0) + band_ref[0] * 8
    order = order_i.astype(F32)
    r = jnp.floor((lane.astype(F32) + 0.5) * (1.0 / LAT))
    row = jnp.minimum(8.0 * (lane.astype(F32) - LAT * r) + r, NLAT - 1.0)
    theta = (row + 0.5) * (math.pi / NLAT)
    cosine, sine = jnp.cos(theta), jnp.sin(theta)
    k = lane.astype(F32) + 1.0
    ratio = jnp.log((2.0 * k - 1.0) / (2.0 * k))
    factor = jnp.sum(jnp.where(k <= order, ratio, 0.0), axis=1, keepdims=True)
    start = 0.5 * jnp.log((2.0 * order + 1.0) / (4.0 * math.pi)) + 0.5 * factor + order * jnp.log(sine)
    square = order * order
    every = 16

    def block(b, carry):
        before, current, log_scale = carry
        scale = jnp.exp(log_scale)
        for t in range(every):
            degree = b * every + t
            l = degree.astype(F32)
            lower = (l - 1.0) * (l - 1.0)
            alpha = jnp.sqrt((4.0 * l * l - 1.0) / jnp.maximum(l * l - square, 1.0))
            beta = jnp.sqrt(jnp.maximum(lower - square, 0.0) / jnp.maximum(4.0 * lower - 1.0, 1.0))
            fresh = (alpha * cosine) * current - (alpha * beta) * before
            fresh = jnp.where(order_i == degree, 1.0, fresh)
            fresh = jnp.where(order_i > degree, 0.0, fresh)
            before, current = current, fresh
            entry = fresh * scale
            for h in range(2):
                table[pl.ds(pl.multiple_of(2048 * h + degree * 8, 8), 8), :] = entry[:, 128 * h : 128 * h + 128]
        largest = jnp.maximum(jnp.abs(before), jnp.abs(current))
        largest = jnp.where(order_i <= b * every + (every - 1), largest, 1.0)
        return before / largest, current / largest, log_scale + jnp.log(largest)

    blank = jnp.zeros(shape, F32)
    lax.fori_loop(0, NLAT // every, block, (blank, blank, start))
    for h in range(2):
        table[2048 * h + NLAT * 8 : 2048 * h + 2048, :] = jnp.zeros((64 * 8, 128), F32)
    weight = jnp.where(lane < NLAT, sine * (math.pi / NLAT), 0.0)[0:1, :]
    for m in range(8):
        p = jnp.concatenate([table[pl.ds(2048 * h + m, 256, stride=8), :] for h in range(2)], axis=1)
        pw_ref[m] = (p * weight).astype(BF)
        pt_ref[m] = jnp.transpose(p)[:NLAT, :].astype(BF)


def spectrum_body(recv_ref, fhi_ref, flo_ref, full_ref, send_ref, first_ref, last_ref, wide):
    wide[...] = recv_ref[...].astype(F32).reshape(LON * 16, 128)
    shape = (LON, 128)
    for e in range(2):
        for h in range(2):
            total = [jnp.zeros(shape, F32)] * PAIRS
            for s in range(4):
                rows = wide[pl.ds(8 * e + 4 * h + s, LON, stride=16), :]
                for q in range(PAIRS):
                    total[q] = jnp.where(inside(shape, 32 * s, CHAN), turn(rows, 32 * s - CHAN * q), total[q])
            for q in range(PAIRS):
                kap = 2 * q + e
                full_ref[32 * kap : 32 * kap + 32, 128 * h : 128 * h + 128] = total[q].astype(BF)
    full = full_ref[...]
    spectrum = jnp.dot(fhi_ref[...], full, preferred_element_type=F32)
    spectrum = spectrum + jnp.dot(flo_ref[...], full, preferred_element_type=F32)
    send_ref[...] = spectrum.astype(BF).reshape(LAT, 16, 256)
    shape = (96, 128)
    for edge_ref, at, own in ((first_ref, 0, 0), (last_ref, 128, 96)):
        edge = jnp.zeros(shape, F32)
        for g in range(4):
            rows = full_ref[96 * g : 96 * g + 96, at : at + 128].astype(F32)
            edge = jnp.where(inside(shape, 32 * g, 32), turn(rows, 32 * g - own), edge)
        edge_ref[...] = edge.astype(BF)


def filter_body(recv_ref, pw_ref, pt_ref, gain_ref, send_ref, wide, out):
    rows = LAT * 16
    for h in range(2):
        wide[rows * h : rows * h + rows, :] = recv_ref[:, :, 128 * h : 128 * h + 128].astype(F32).reshape(rows, 128)
    gain = gain_ref[...]
    shape = (LAT, 128)
    lane = lanes_of(shape)
    for m in range(8):
        chunks = []
        for h in range(2):
            low, high = (wide[pl.ds(rows * h + 8 * p + m, LAT, stride=16), :] for p in range(2))
            for s in range(4):
                chunks.append(jnp.where(lane < 32, turn(low, -32 * s), turn(high, 32 - 32 * s)))
        chunks.append(jnp.zeros((256 - NLAT, 128), F32))
        field = jnp.concatenate(chunks, axis=0).astype(BF)
        coefficients = jnp.dot(pw_ref[m], field, preferred_element_type=F32) * gain
        back = jnp.dot(pt_ref[m], coefficients.astype(BF), preferred_element_type=F32)
        for p in range(2):
            for h in range(2):
                total = jnp.zeros(shape, F32)
                for s in range(4):
                    r = 4 * h + s
                    total = jnp.where(
                        inside(shape, 32 * s, 32), turn(back[LAT * r : LAT * r + LAT, :], 32 * s - 32 * p), total
                    )
                out[pl.ds(rows * h + 8 * p + m, LAT, stride=16), :] = total
    for h in range(2):
        send_ref[:, :, 128 * h : 128 * h + 128] = out[rows * h : rows * h + rows, :].astype(BF).reshape(LAT, 16, 128)


def local_body(full_ref, above_ref, below_ref, taps_ref, base_ref, up, down):
    shape = (96, 128)
    lane = lanes_of(shape)
    for g in range(4):
        at = slice(96 * g, 96 * g + 96)
        left, right = full_ref[at, 0:128].astype(F32), full_ref[at, 128:256].astype(F32)
        above, below = above_ref[...].astype(F32), below_ref[...].astype(F32)
        up[at, 0:128] = jnp.where(lane < 32, turn(above, -32 * g), turn(left, 32))
        up[at, 128:256] = jnp.where(lane < 32, turn(left, 32), turn(right, 32))
        down[at, 0:128] = jnp.where(lane >= 96, turn(right, 96), turn(left, 96))
        down[at, 128:256] = jnp.where(lane >= 96, turn(below, 96 - 32 * g), turn(right, 96))

    def mixed(kap, b):
        at = slice(32 * kap, 32 * kap + 32)
        rows = (up[at, :], full_ref[at, :].astype(F32), down[at, :])
        return sum(taps_ref[3 * i + b : 3 * i + b + 1, :] * rows[i] for i in range(3))

    for kap in range(COLS):
        west = mixed(kap - 1, 0) if kap > 0 else pltpu.roll(mixed(COLS - 1, 0), 1, 0)
        east = mixed(kap + 1, 2) if kap < COLS - 1 else pltpu.roll(mixed(0, 2), LON - 1, 0)
        at = slice(32 * kap, 32 * kap + 32)
        base_ref[at, :] = full_ref[at, :].astype(F32) + (west + mixed(kap, 1) + east)


def synthesis_body(recv_ref, ihi_ref, ilo_ref, base_ref, send_ref, out):
    modes = recv_ref[...].reshape(NLON, 256)
    summed = jnp.dot(ihi_ref[...], modes, preferred_element_type=F32)
    summed = base_ref[...] + (summed + jnp.dot(ilo_ref[...], modes, preferred_element_type=F32))
    shape = (LON, 128)
    for e in range(2):
        for h in range(2):
            for s in range(4):
                total = jnp.zeros(shape, F32)
                for q in range(PAIRS):
                    kap = 2 * q + e
                    rows = summed[32 * kap : 32 * kap + 32, 128 * h : 128 * h + 128]
                    total = jnp.where(inside(shape, CHAN * q, CHAN), turn(rows, CHAN * q - 32 * s), total)
                out[pl.ds(8 * e + 4 * h + s, LON, stride=16), :] = total
    send_ref[...] = out[...].astype(BF).reshape(LON, 16, 128)


def mlp_body(recv_ref, gain_ref, win_ref, wout_ref, out_ref, summed_ref):
    shape = (16, 128)
    lane = lanes_of(shape)
    for tile in range(5):
        for q in range(PAIRS):
            total = jnp.zeros(shape, F32)
            for d in range(128 * tile // CHAN, (128 * tile + 127) // CHAN + 1):
                off = CHAN * d - 128 * tile
                piece = turn(recv_ref[d].astype(F32), off - CHAN * q)
                total = jnp.where((lane >= off) & (lane < off + CHAN), piece, total)
            summed_ref[16 * q : 16 * q + 16, 128 * tile : 128 * tile + 128] = total
    summed = summed_ref[...]
    mean = jnp.sum(summed * summed, axis=1, keepdims=True) * (1.0 / summed.shape[1])
    normed = (summed * lax.rsqrt(mean + EPS) * gain_ref[...]).astype(BF)
    hidden = jnp.dot(normed, win_ref[...], preferred_element_type=F32)
    hidden = (0.5 * hidden * (1.0 + lax.erf(hidden * math.sqrt(0.5)))).astype(BF)
    result = summed + jnp.dot(hidden, wout_ref[...], preferred_element_type=F32)
    out_ref[...] = result.astype(BF)


def on_device(latent_field, spectral_filter, conv_weight, norm_gain, weight_in, weight_out):
    channels = latent_field.shape[0]
    field = jnp.transpose(latent_field, (2, 1, 0)).reshape(COLS * ROWS, channels)
    pieces = call(pack_body, ((LON, 16, 128), BF), field, name="pack")
    pieces = lax.all_to_all(pieces, "lon", 0, 0, tiled=True)

    fhi, flo, ihi, ilo = call(fourier_body, [((NLON, NLON), BF)] * 4, name="fourier_tables", flops=10_000_000)
    band = lax.axis_index("lat").astype(jnp.int32).reshape(1)
    pw, pt = call(
        legendre_body,
        [((8, 256, 256), BF), ((8, NLAT, 256), BF)],
        band,
        scratch=[pltpu.VMEM((2 * 2048, 128), F32)],
        in_specs=[pl.BlockSpec(memory_space=pltpu.SMEM)],
        name="legendre_tables",
        flops=10_000_000,
    )
    gain = jnp.pad(jnp.transpose(spectral_filter), ((0, 64), (0, 32 - CHAN)))
    gain = jnp.tile(gain, (1, 4))
    taps = lax.dynamic_slice_in_dim(conv_weight, lax.axis_index("lon") * CHAN, CHAN, 1)
    taps = jnp.tile(jnp.pad(taps, ((0, 7), (0, 32 - CHAN))), (1, 8))

    full, modes, first, last = call(
        spectrum_body,
        [((NLON, 256), BF), ((LAT, 16, 256), BF), ((96, 128), BF), ((96, 128), BF)],
        pieces,
        fhi,
        flo,
        scratch=[pltpu.VMEM((LON * 16, 128), F32)],
        name="spectrum",
    )
    modes = lax.all_to_all(modes, "lat", 0, 0, tiled=True)
    below = lax.ppermute(first, "lat", [(i + 1, i) for i in range(LAT - 1)])
    above = lax.ppermute(last, "lat", [(i, i + 1) for i in range(LAT - 1)])
    modes = call(
        filter_body,
        ((LAT, 16, 256), BF),
        modes,
        pw,
        pt,
        gain,
        scratch=[pltpu.VMEM((2 * LAT * 16, 128), F32)] * 2,
        name="filter",
    )
    modes = lax.all_to_all(modes, "lat", 0, 0, tiled=True)
    base = call(
        local_body,
        ((NLON, 256), F32),
        full,
        above,
        below,
        taps,
        scratch=[pltpu.VMEM((NLON, 256), F32)] * 2,
        name="local_mix",
        flops=5_000_000,
    )
    pieces = call(
        synthesis_body,
        ((LON, 16, 128), BF),
        modes,
        ihi,
        ilo,
        base,
        scratch=[pltpu.VMEM((LON * 16, 128), F32)],
        name="synthesis",
    )
    pieces = lax.all_to_all(pieces, "lon", 0, 0, tiled=True)
    result = call(
        mlp_body,
        ((COLS * ROWS, channels), BF),
        pieces,
        norm_gain.reshape(1, channels),
        weight_in,
        weight_out,
        scratch=[pltpu.VMEM((COLS * ROWS, channels), F32)],
        name="mlp",
    )
    return jnp.transpose(result.reshape(COLS, ROWS, channels), (2, 1, 0))


def solution(mesh):
    in_specs = (P(None, "lat", "lon"), P("lon", None), P(), P(), P(), P())
    return jax.shard_map(on_device, mesh=mesh, in_specs=in_specs, out_specs=P(None, "lat", "lon"), check_vma=False)
```

```python
import math

import jax
import jax.numpy as jnp
from jax import lax
from jax.experimental import pallas as pl
from jax.experimental.pallas import tpu as pltpu
from jax.sharding import PartitionSpec as P

LON, LAT, COLS, ROWS, CHAN = 32, 24, 12, 8, 20
NLON, NLAT = LON * COLS, LAT * ROWS
PAIRS = COLS // 2
BF, F32 = jnp.bfloat16, jnp.float32
EPS = 1e-06
SLOTS = [*range(LAT // 2), *range(LAT - 1, LAT // 2 - 1, -1)]


def lanes_of(shape):
    return lax.broadcasted_iota(jnp.int32, shape, 1)


def inside(shape, start, width):
    lane = lanes_of(shape)
    return (lane >= start) & (lane < start + width)


def turn(x, shift):
    shift %= 128
    return x if shift == 0 else pltpu.roll(x, shift, 1)


VMEM, HBM, ANY, SMEM = pltpu.VMEM, pltpu.HBM, pl.ANY, pltpu.SMEM


def call(body, outs, args, scratch=(), name=None, mib=24, flops=0):
    result = pl.pallas_call(
        body,
        out_shape=[
            HBM(shape, kind) if space is HBM else jax.ShapeDtypeStruct(shape, kind) for shape, kind, space in outs
        ],
        in_specs=[pl.BlockSpec(memory_space=space) for _, space in args],
        out_specs=[pl.BlockSpec(memory_space=space) for _, _, space in outs],
        scratch_shapes=list(scratch),
        compiler_params=pltpu.CompilerParams(vmem_limit_bytes=mib * 2**20),
        cost_estimate=pl.CostEstimate(flops=flops, bytes_accessed=1_000_000, transcendentals=0),
        name=name,
    )(*(pltpu.with_memory_space_constraint(array, HBM) if space is HBM else array for array, space in args))
    return result[0] if len(outs) == 1 else result


def swap_halves(x):
    return pltpu.roll(x, LAT // 2, 0)


def begin(source, target, sem):
    copy = pltpu.make_async_copy(source, target, sem)
    copy.start()
    return copy


def pack_body(field_ref, out_ref, x_ref, send_ref, sems):
    shape = (16, 128)
    begin(field_ref, x_ref, sems.at[4]).wait()
    copies = []
    for d in range(LON):
        tile, off = divmod(CHAN * d, 128)
        last = (CHAN * d + CHAN - 1) // 128
        total = jnp.zeros(shape, F32)
        for q in range(PAIRS):
            at = slice(16 * q, 16 * q + 16)
            piece = x_ref[at, 128 * tile : 128 * tile + 128].astype(F32)
            if last > tile:
                after = x_ref[at, 128 * last : 128 * last + 128].astype(F32)
                piece = jnp.where(lanes_of(shape) >= off, piece, after)
            total = jnp.where(inside(shape, CHAN * q, CHAN), turn(piece, CHAN * q - off), total)
        send_ref[d] = total.astype(BF)
        if d % 8 == 7:
            at = pl.ds(d - 7, 8)
            copies.append(begin(send_ref.at[at], out_ref.at[at], sems.at[d // 8]))
    for copy in copies:
        copy.wait()


def wave(order, part, column):
    v = (order * column + part * (NLON // 4)).astype(F32)
    index = v - NLON * jnp.floor(v * (1.0 / NLON))
    x = (NLON // 4 - jnp.abs(index - NLON // 2)) * (2.0 * math.pi / NLON)
    y = x * x
    s = 1.0 / 6227020800.0
    for term in (-1.0 / 39916800.0, 1.0 / 362880.0, -1.0 / 5040.0, 1.0 / 120.0, -1.0 / 6.0, 1.0):
        s = s * y + term
    return -(s * x)


def mode_of(n):
    slot = n >> 4
    device = jnp.where(slot < LAT // 2, slot, LAT + LAT // 2 - 1 - slot)
    return (device << 3) + (n & 7), (n >> 3) & 1


def column_of(k):
    return COLS * (k & 31) + (k >> 5)


def halves(x):
    high = x.astype(BF)
    return high, (x - high.astype(F32)).astype(BF)


def fourier_body(sector_ref, kernel_ref, fhi_ref, flo_ref, taps_ref):
    shape = (16, NLON)
    lane = lanes_of(shape)

    def block(b, unused):
        row = lax.broadcasted_iota(jnp.int32, shape, 0) + 16 * b
        at = pl.ds(pl.multiple_of(16 * b, 16), 16)
        order, part = mode_of(row)
        table = wave(order, part, column_of(lane)) * (2.0 * math.pi / NLON)
        fhi_ref[at, :], flo_ref[at, :] = halves(table)
        return unused

    lax.fori_loop(0, NLON // 16, block, 0)
    wide = (kernel_ref.shape[1], 256)
    own = lanes_of(wide) & 31
    channel = lax.broadcasted_iota(jnp.int32, wide, 0)
    picked = (channel == own + sector_ref[0] * CHAN) & (own < CHAN)
    taps_ref[0:9, :] = jnp.dot(
        kernel_ref[...], jnp.where(picked, 1.0, 0.0), precision=lax.Precision.HIGHEST, preferred_element_type=F32
    )


def legendre_body(band_ref, p_out, pt_out, table, p_ref, pt_ref, sems):
    shape = (8, 128)
    lane = lanes_of(shape)
    order_i = lax.broadcasted_iota(jnp.int32, shape, 0) + band_ref[0] * 8
    order = order_i.astype(F32)
    r = jnp.floor((lane.astype(F32) + 0.5) * (1.0 / LAT))
    slot = lane.astype(F32) - LAT * r
    device = jnp.where(slot < LAT // 2, slot, LAT + LAT // 2 - 1.0 - slot)
    row = jnp.minimum(8.0 * device + r, NLAT - 1.0)
    theta = (row + 0.5) * (math.pi / NLAT)
    cosine, sine = jnp.cos(theta), jnp.sin(theta)
    k = lanes_of((8, 256)).astype(F32) + 1.0
    ratio = jnp.log((2.0 * k - 1.0) / (2.0 * k))
    factor = jnp.sum(jnp.where(k <= order[:, 0:1], ratio, 0.0), axis=1, keepdims=True)
    start = 0.5 * jnp.log((2.0 * order + 1.0) / (4.0 * math.pi)) + 0.5 * factor + order * jnp.log(sine)
    square = order * order
    every = 16

    def block(b, carry):
        before, current, log_scale = carry
        scale = jnp.exp(log_scale)
        for t in range(every):
            degree = b * every + t
            l = degree.astype(F32)
            lower = (l - 1.0) * (l - 1.0)
            alpha = jnp.sqrt((4.0 * l * l - 1.0) / jnp.maximum(l * l - square, 1.0))
            beta = jnp.sqrt(jnp.maximum(lower - square, 0.0) / jnp.maximum(4.0 * lower - 1.0, 1.0))
            fresh = (alpha * cosine) * current - (alpha * beta) * before
            fresh = jnp.where(order_i == degree, 1.0, fresh)
            fresh = jnp.where(order_i > degree, 0.0, fresh)
            before, current = current, fresh
            table[pl.ds(pl.multiple_of(degree * 8, 8), 8), :] = fresh * scale
        largest = jnp.maximum(jnp.abs(before), jnp.abs(current))
        largest = jnp.where(order_i <= b * every + (every - 1), largest, 1.0)
        return before / largest, current / largest, log_scale + jnp.log(largest)

    blank = jnp.zeros(shape, F32)
    lax.fori_loop(0, NLAT // every, block, (blank, blank, start))
    copies = []
    blank = jnp.zeros((128 - NLAT // 2, 128), F32)
    for m in range(8):
        for parity in range(2):
            p = jnp.where(lanes_of((96, 128)) < 96, table[pl.ds(8 * parity + m, 96, stride=16), :], 0.0)
            p_ref[m, 96 * parity : 96 * parity + 96, :] = p.astype(BF)
            turned = jnp.transpose(jnp.concatenate([p, blank], axis=0))
            pt_ref[m, 96 * parity : 96 * parity + 96, :] = turned[:96, :].astype(BF)
        if m % 4 == 3:
            at = pl.ds(m - 3, 4)
            copies.append(begin(p_ref.at[at], p_out.at[at], sems.at[m // 4]))
            copies.append(begin(pt_ref.at[at], pt_out.at[at], sems.at[2 + m // 4]))
    for copy in copies:
        copy.wait()


def spectrum_body(
    band_ref, recv_ref, fhi_ref, flo_ref, send_out, full_out, first_out, last_out, wide, full_ref, send_ref, edge_ref, sems
):
    wide[...] = recv_ref[...].astype(F32).reshape(LON * 16, 128)
    shape = (LON, 128)
    for e in range(2):
        for h in range(2):
            total = [jnp.zeros(shape, F32)] * PAIRS
            for s in range(4):
                rows = wide[pl.ds(8 * e + 4 * h + s, LON, stride=16), :]
                for q in range(PAIRS):
                    total[q] = jnp.where(inside(shape, 32 * s, CHAN), turn(rows, 32 * s - CHAN * q), total[q])
            for q in range(PAIRS):
                kap = 2 * q + e
                full_ref[32 * kap : 32 * kap + 32, 128 * h : 128 * h + 128] = total[q].astype(BF)
    copies = [begin(full_ref, full_out, sems.at[1])]
    full = full_ref[...]
    spectrum = jnp.dot(fhi_ref[...], full, preferred_element_type=F32)
    spectrum = spectrum + jnp.dot(flo_ref[...], full, preferred_element_type=F32)
    row = (lanes_of((1, 256)) >> 5) + band_ref[0] * ROWS
    weight = jnp.sin((row.astype(F32) + 0.5) * (math.pi / NLAT)) * (math.pi / NLAT)
    send_ref[...] = (spectrum * weight).astype(BF).reshape(LAT, 16, 256)
    copies.append(begin(send_ref, send_out, sems.at[0]))
    shape = (96, 128)
    for i, (edge_out, at, own) in enumerate(((first_out, 0, 0), (last_out, 128, 96))):
        edge = jnp.zeros(shape, F32)
        for g in range(4):
            rows = full_ref[96 * g : 96 * g + 96, at : at + 128].astype(F32)
            edge = jnp.where(inside(shape, 32 * g, 32), turn(rows, 32 * g - own), edge)
        edge_ref[i] = edge.astype(BF)
        copies.append(begin(edge_ref.at[i], edge_out, sems.at[2 + i]))
    for copy in copies:
        copy.wait()


def filter_body(recv_ref, p_in, pt_in, gain_in, send_out, wide, out, p_ref, pt_ref, gain_ref, send_ref, sems):
    cuts = [pl.ds(4 * i, 4) for i in range(2)]
    tables = []
    for i, at in enumerate(cuts):
        tables.append([begin(p_in.at[at], p_ref.at[at], sems.at[2 * i])])
        if i == 0:
            tables[0].append(begin(gain_in, gain_ref, sems.at[4]))
        tables[i].append(begin(pt_in.at[at], pt_ref.at[at], sems.at[2 * i + 1]))
    rows = LAT * 16
    for h in range(2):
        wide[rows * h : rows * h + rows, :] = recv_ref[:, :, 128 * h : 128 * h + 128].astype(F32).reshape(rows, 128)
    shape = (LAT, 128)
    lane = lanes_of(shape)
    blank = jnp.zeros((32, 128), F32)
    for m in range(8):
        chunks = []
        for h in range(2):
            low, high = (wide[pl.ds(rows * h + 8 * p + m, LAT, stride=16), :] for p in range(2))
            for s in range(4):
                chunks.append(jnp.where(lane < 32, turn(low, -32 * s), turn(high, 32 - 32 * s)))
        mirrored = [swap_halves(chunks[7 - r]) for r in range(4)]
        even = jnp.concatenate([chunks[r] + mirrored[r] for r in range(4)] + [blank], axis=0).astype(BF)
        odd = jnp.concatenate([chunks[r] - mirrored[r] for r in range(4)] + [blank], axis=0).astype(BF)
        if m % 4 == 0:
            for copy in tables[m // 4]:
                copy.wait()
        halves_back = []
        for parity in range(2):
            at = slice(96 * parity, 96 * parity + 96)
            field = even if (parity + m) % 2 == 0 else odd
            scaled = jnp.dot(p_ref[m, at, :], field, preferred_element_type=F32)
            scaled = scaled * gain_ref[pl.ds(parity, 96, stride=2), :]
            scaled = jnp.concatenate([scaled, blank], axis=0).astype(BF)
            halves_back.append(jnp.dot(pt_ref[m, at, :], scaled, preferred_element_type=F32))
        if m % 2 == 1:
            halves_back.reverse()
        near, far = halves_back[0] + halves_back[1], halves_back[0] - halves_back[1]
        back = [near[LAT * r : LAT * r + LAT, :] for r in range(4)]
        back = back + [swap_halves(far[LAT * r : LAT * r + LAT, :]) for r in (3, 2, 1, 0)]
        for p in range(2):
            for h in range(2):
                total = jnp.zeros(shape, F32)
                for s in range(4):
                    r = 4 * h + s
                    total = jnp.where(
                        inside(shape, 32 * s, 32), turn(back[r], 32 * s - 32 * p), total
                    )
                out[pl.ds(rows * h + 8 * p + m, LAT, stride=16), :] = total
    for h in range(2):
        send_ref[:, :, 128 * h : 128 * h + 128] = out[rows * h : rows * h + rows, :].astype(BF).reshape(LAT, 16, 128)
    begin(send_ref, send_out, sems.at[5]).wait()


def local_body(full_in, above_ref, below_ref, taps_ref, base_out, full_ref, base_ref, up, down, sems):
    begin(full_in, full_ref, sems.at[0]).wait()
    shape = (96, 128)
    lane = lanes_of(shape)
    for g in range(4):
        at = slice(96 * g, 96 * g + 96)
        left, right = full_ref[at, 0:128].astype(F32), full_ref[at, 128:256].astype(F32)
        above, below = above_ref[...].astype(F32), below_ref[...].astype(F32)
        up[at, 0:128] = jnp.where(lane < 32, turn(above, -32 * g), turn(left, 32))
        up[at, 128:256] = jnp.where(lane < 32, turn(left, 32), turn(right, 32))
        down[at, 0:128] = jnp.where(lane >= 96, turn(right, 96), turn(left, 96))
        down[at, 128:256] = jnp.where(lane >= 96, turn(below, 96 - 32 * g), turn(right, 96))

    def mixed(kap, b):
        at = slice(32 * kap, 32 * kap + 32)
        rows = (up[at, :], full_ref[at, :].astype(F32), down[at, :])
        return sum(taps_ref[3 * i + b : 3 * i + b + 1, :] * rows[i] for i in range(3))

    for kap in range(COLS):
        west = mixed(kap - 1, 0) if kap > 0 else pltpu.roll(mixed(COLS - 1, 0), 1, 0)
        east = mixed(kap + 1, 2) if kap < COLS - 1 else pltpu.roll(mixed(0, 2), LON - 1, 0)
        at = slice(32 * kap, 32 * kap + 32)
        base_ref[at, :] = (full_ref[at, :].astype(F32) + (west + mixed(kap, 1) + east)).astype(BF)
    begin(base_ref, base_out, sems.at[1]).wait()


def synthesis_body(recv_ref, base_in, send_out, inv_ref, base_ref, send_ref, out, summed_ref, sems):
    base = begin(base_in, base_ref, sems.at[0])
    shape = (LON, NLON)
    order, part = mode_of(lanes_of(shape))
    column = COLS * lax.broadcasted_iota(jnp.int32, shape, 0)
    weight = jnp.where(order == 0, 1.0, 2.0)
    cosine, sine = wave(order, part, column) * weight, wave(order, part + 1, column) * weight
    shape = (16, NLON)
    order, _ = mode_of(lanes_of(shape))
    column = lax.broadcasted_iota(jnp.int32, shape, 0)
    step_cosine, step_sine = wave(order, 0, column), wave(order, 1, column)
    for kap in range(COLS):
        turned = cosine * step_cosine[kap : kap + 1, :] - sine * step_sine[kap : kap + 1, :]
        inv_ref[32 * kap : 32 * kap + 32, :] = turned.astype(BF)
    summed_ref[...] = jnp.dot(inv_ref[...], recv_ref[...].reshape(NLON, 256), preferred_element_type=F32)
    base.wait()
    summed_ref[...] += base_ref[...].astype(F32)
    shape = (LON, 128)
    for e in range(2):
        for h in range(2):
            for s in range(4):
                total = jnp.zeros(shape, F32)
                for q in range(PAIRS):
                    kap = 2 * q + e
                    rows = summed_ref[32 * kap : 32 * kap + 32, 128 * h : 128 * h + 128]
                    total = jnp.where(inside(shape, CHAN * q, CHAN), turn(rows, CHAN * q - 32 * s), total)
                out[pl.ds(8 * e + 4 * h + s, LON, stride=16), :] = total
    send_ref[...] = out[...].astype(BF).reshape(LON, 16, 128)
    begin(send_ref, send_out, sems.at[1]).wait()


def mlp_body(recv_ref, gain_ref, win_ref, wout_ref, out_ref, summed_ref):
    shape = (16, 128)
    lane = lanes_of(shape)
    for tile in range(5):
        for q in range(PAIRS):
            total = jnp.zeros(shape, F32)
            for d in range(128 * tile // CHAN, (128 * tile + 127) // CHAN + 1):
                off = CHAN * d - 128 * tile
                piece = turn(recv_ref[d].astype(F32), off - CHAN * q)
                total = jnp.where((lane >= off) & (lane < off + CHAN), piece, total)
            summed_ref[16 * q : 16 * q + 16, 128 * tile : 128 * tile + 128] = total
    summed = summed_ref[...]
    mean = jnp.sum(summed * summed, axis=1, keepdims=True) * (1.0 / summed.shape[1])
    normed = (summed * lax.rsqrt(mean + EPS) * gain_ref[...]).astype(BF)
    hidden = jnp.dot(normed, win_ref[...], preferred_element_type=F32)
    hidden = (0.5 * hidden * (1.0 + lax.erf(hidden * math.sqrt(0.5)))).astype(BF)
    result = summed + jnp.dot(hidden, wout_ref[...], preferred_element_type=F32)
    out_ref[...] = result.astype(BF)


def on_device(latent_field, spectral_filter, conv_weight, norm_gain, weight_in, weight_out):
    channels = latent_field.shape[0]
    points = COLS * ROWS
    table, circle, group, mode = (NLON, NLON), (NLON, 256), (LON, 16, 128), (LAT, 16, 256)
    field = jnp.transpose(latent_field, (2, 1, 0)).reshape(points, channels)
    pieces = call(
        pack_body,
        [(group, BF, HBM)],
        [(field, HBM)],
        [VMEM((points, channels), BF), VMEM(group, BF), pltpu.SemaphoreType.DMA((5,))],
        name="pack",
    )
    pieces = lax.all_to_all(pieces, "lon", 0, 0, tiled=True)

    sector = lax.axis_index("lon").astype(jnp.int32).reshape(1)
    band = lax.axis_index("lat").astype(jnp.int32).reshape(1)
    fhi, flo, taps = call(
        fourier_body,
        [(table, BF, VMEM), (table, BF, VMEM), ((16, 256), F32, VMEM)],
        [(sector, SMEM), (conv_weight, VMEM)],
        name="fourier_tables",
        flops=10_000_000,
    )
    modes, full, first, last = call(
        spectrum_body,
        [(mode, BF, HBM), (circle, BF, HBM), ((96, 128), BF, HBM), ((96, 128), BF, HBM)],
        [(band, SMEM), (pieces, VMEM), (fhi, VMEM), (flo, VMEM)],
        [VMEM((LON * 16, 128), F32), VMEM(circle, BF), VMEM(mode, BF), VMEM((2, 96, 128), BF), pltpu.SemaphoreType.DMA((4,))],
        name="spectrum",
    )
    modes = lax.all_to_all(modes, "lat", 0, 0, tiled=True, axis_index_groups=[SLOTS])
    polynomials = (8, NLAT, 128)
    p, pt = call(
        legendre_body,
        [(polynomials, BF, HBM)] * 2,
        [(band, SMEM)],
        [VMEM((NLAT * 8, 128), F32), VMEM(polynomials, BF), VMEM(polynomials, BF), pltpu.SemaphoreType.DMA((4,))],
        name="legendre_tables",
        flops=10_000_000,
    )
    gain = jnp.tile(jnp.pad(jnp.transpose(spectral_filter), ((0, 0), (0, 32 - CHAN))), (1, 4))
    modes = call(
        filter_body,
        [(mode, BF, HBM)],
        [(modes, VMEM), (p, HBM), (pt, HBM), (gain, HBM)],
        [VMEM((2 * LAT * 16, 128), F32)] * 2
        + [VMEM(polynomials, BF)] * 2
        + [VMEM((NLAT, 128), F32), VMEM(mode, BF), pltpu.SemaphoreType.DMA((6,))],
        name="filter",
    )
    modes = lax.all_to_all(modes, "lat", 0, 0, tiled=True, axis_index_groups=[SLOTS])
    below = lax.ppermute(first, "lat", [(i + 1, i) for i in range(LAT - 1)])
    above = lax.ppermute(last, "lat", [(i, i + 1) for i in range(LAT - 1)])
    base = call(
        local_body,
        [(circle, BF, HBM)],
        [(full, HBM), (above, VMEM), (below, VMEM), (taps, VMEM)],
        [VMEM(circle, BF)] * 2 + [VMEM(circle, F32)] * 2 + [pltpu.SemaphoreType.DMA((2,))],
        name="local_mix",
        flops=5_000_000,
    )
    pieces = call(
        synthesis_body,
        [(group, BF, HBM)],
        [(modes, VMEM), (base, HBM)],
        [VMEM(table, BF), VMEM(circle, BF), VMEM(group, BF), VMEM((LON * 16, 128), F32), VMEM(circle, F32)]
        + [pltpu.SemaphoreType.DMA((2,))],
        name="synthesis",
    )
    pieces = lax.all_to_all(pieces, "lon", 0, 0, tiled=True)
    result = call(
        mlp_body,
        [((points, channels), BF, VMEM)],
        [(pieces, VMEM), (norm_gain.reshape(1, channels), VMEM), (weight_in, VMEM), (weight_out, VMEM)],
        [VMEM((points, channels), F32)],
        name="mlp",
    )
    return jnp.transpose(result.reshape(COLS, ROWS, channels), (2, 1, 0))


def solution(mesh):
    in_specs = (P(None, "lat", "lon"), P("lon", None), P(), P(), P(), P())
    return jax.shard_map(on_device, mesh=mesh, in_specs=in_specs, out_specs=P(None, "lat", "lon"), check_vma=False)
```

```python
import math

import jax
import jax.numpy as jnp
from jax import lax
from jax.experimental import pallas as pl
from jax.experimental.pallas import tpu as pltpu
from jax.sharding import PartitionSpec as P

LON, LAT, COLS, ROWS, CHAN = 32, 24, 12, 8, 20
NLON, NLAT = LON * COLS, LAT * ROWS
PAIRS = COLS // 2
BF, F32 = jnp.bfloat16, jnp.float32
EPS = 1e-06
SLOTS = [*range(LAT // 2), *range(LAT - 1, LAT // 2 - 1, -1)]


def lanes_of(shape):
    return lax.broadcasted_iota(jnp.int32, shape, 1)


def inside(shape, start, width):
    lane = lanes_of(shape)
    return (lane >= start) & (lane < start + width)


def turn(x, shift):
    shift %= 128
    return x if shift == 0 else pltpu.roll(x, shift, 1)


VMEM, HBM, ANY, SMEM = pltpu.VMEM, pltpu.HBM, pl.ANY, pltpu.SMEM


def call(body, outs, args, scratch=(), name=None, mib=24, flops=0):
    result = pl.pallas_call(
        body,
        out_shape=[
            HBM(shape, kind) if space is HBM else jax.ShapeDtypeStruct(shape, kind) for shape, kind, space in outs
        ],
        in_specs=[pl.BlockSpec(memory_space=space) for _, space in args],
        out_specs=[pl.BlockSpec(memory_space=space) for _, _, space in outs],
        scratch_shapes=list(scratch),
        compiler_params=pltpu.CompilerParams(vmem_limit_bytes=mib * 2**20),
        cost_estimate=pl.CostEstimate(flops=flops, bytes_accessed=1_000_000, transcendentals=0),
        name=name,
    )(*(pltpu.with_memory_space_constraint(array, HBM) if space is HBM else array for array, space in args))
    return result[0] if len(outs) == 1 else result


def swap_halves(x):
    return pltpu.roll(x, LAT // 2, 0)


def begin(source, target, sem):
    copy = pltpu.make_async_copy(source, target, sem)
    copy.start()
    return copy


def pack_body(field_ref, out_ref, x_ref, send_ref, sems):
    shape = (16, 128)
    begin(field_ref, x_ref, sems.at[4]).wait()
    copies = []
    for d in range(LON):
        tile, off = divmod(CHAN * d, 128)
        last = (CHAN * d + CHAN - 1) // 128
        total = jnp.zeros(shape, F32)
        for q in range(PAIRS):
            at = slice(16 * q, 16 * q + 16)
            piece = x_ref[at, 128 * tile : 128 * tile + 128].astype(F32)
            if last > tile:
                after = x_ref[at, 128 * last : 128 * last + 128].astype(F32)
                piece = jnp.where(lanes_of(shape) >= off, piece, after)
            total = jnp.where(inside(shape, CHAN * q, CHAN), turn(piece, CHAN * q - off), total)
        send_ref[d] = total.astype(BF)
        if d % 8 == 7:
            at = pl.ds(d - 7, 8)
            copies.append(begin(send_ref.at[at], out_ref.at[at], sems.at[d // 8]))
    for copy in copies:
        copy.wait()


def wave(order, part, column):
    v = (order * column + part * (NLON // 4)).astype(F32)
    index = v - NLON * jnp.floor(v * (1.0 / NLON))
    x = (NLON // 4 - jnp.abs(index - NLON // 2)) * (2.0 * math.pi / NLON)
    y = x * x
    s = 1.0 / 6227020800.0
    for term in (-1.0 / 39916800.0, 1.0 / 362880.0, -1.0 / 5040.0, 1.0 / 120.0, -1.0 / 6.0, 1.0):
        s = s * y + term
    return -(s * x)


def mode_of(n):
    slot = n >> 4
    device = jnp.where(slot < LAT // 2, slot, LAT + LAT // 2 - 1 - slot)
    order, part = (device << 3) + (n & 7), (n >> 3) & 1
    highest = (order == 0) & (part == 1)
    return jnp.where(highest, NLON // 2, order), jnp.where(highest, 0, part)


def column_of(k):
    return COLS * (k & 31) + (k >> 5)


def halves(x):
    high = x.astype(BF)
    return high, (x - high.astype(F32)).astype(BF)


def fourier_body(sector_ref, kernel_in, fhi_ref, flo_ref, taps_ref, kernel_ref, sem):
    arriving = begin(kernel_in, kernel_ref, sem)
    shape = (16, NLON)
    lane = lanes_of(shape)

    def block(b, unused):
        row = lax.broadcasted_iota(jnp.int32, shape, 0) + 16 * b
        at = pl.ds(pl.multiple_of(16 * b, 16), 16)
        order, part = mode_of(row)
        table = wave(order, part, column_of(lane)) * (2.0 * math.pi / NLON)
        fhi_ref[at, :], flo_ref[at, :] = halves(table)
        return unused

    lax.fori_loop(0, NLON // 16, block, 0)
    arriving.wait()
    wide = (kernel_ref.shape[1], 256)
    own = lanes_of(wide) & 31
    channel = lax.broadcasted_iota(jnp.int32, wide, 0)
    picked = (channel == own + sector_ref[0] * CHAN) & (own < CHAN)
    taps_ref[0:9, :] = jnp.dot(
        kernel_ref[...], jnp.where(picked, 1.0, 0.0), precision=lax.Precision.HIGHEST, preferred_element_type=F32
    )


def legendre_body(
    band_ref, gain_in, p_out, pt_out, gain_out, table, p_ref, pt_ref, gain_ref, own_ref, square_ref, sems
):
    arriving = begin(gain_in, own_ref, sems.at[4])
    shape = (8, 128)
    lane = lanes_of(shape)
    order_i = lax.broadcasted_iota(jnp.int32, shape, 0) + band_ref[0] * 8
    order = order_i.astype(F32)
    r = jnp.floor((lane.astype(F32) + 0.5) * (1.0 / LAT))
    slot = lane.astype(F32) - LAT * r
    device = jnp.where(slot < LAT // 2, slot, LAT + LAT // 2 - 1.0 - slot)
    row = jnp.minimum(8.0 * device + r, NLAT - 1.0)
    theta = (row + 0.5) * (math.pi / NLAT)
    cosine, sine = jnp.cos(theta), jnp.sin(theta)
    k = lanes_of((8, 256)).astype(F32) + 1.0
    ratio = jnp.log((2.0 * k - 1.0) / (2.0 * k))
    factor = jnp.sum(jnp.where(k <= order[:, 0:1], ratio, 0.0), axis=1, keepdims=True)
    start = 0.5 * jnp.log((2.0 * order + 1.0) / (4.0 * math.pi)) + 0.5 * factor + order * jnp.log(sine)
    square = order * order
    every = 16

    def block(b, carry):
        before, current, log_scale = carry
        scale = jnp.exp(log_scale)
        for t in range(every):
            degree = b * every + t
            l = degree.astype(F32)
            lower = (l - 1.0) * (l - 1.0)
            alpha = jnp.sqrt((4.0 * l * l - 1.0) / jnp.maximum(l * l - square, 1.0))
            beta = jnp.sqrt(jnp.maximum(lower - square, 0.0) / jnp.maximum(4.0 * lower - 1.0, 1.0))
            fresh = (alpha * cosine) * current - (alpha * beta) * before
            fresh = jnp.where(order_i == degree, 1.0, fresh)
            fresh = jnp.where(order_i > degree, 0.0, fresh)
            before, current = current, fresh
            table[pl.ds(pl.multiple_of(degree * 8, 8), 8), :] = fresh * scale
        largest = jnp.maximum(jnp.abs(before), jnp.abs(current))
        largest = jnp.where(order_i <= b * every + (every - 1), largest, 1.0)
        return before / largest, current / largest, log_scale + jnp.log(largest)

    blank = jnp.zeros(shape, F32)
    lax.fori_loop(0, NLAT // every, block, (blank, blank, start))
    copies = []
    arriving.wait()
    square_ref[0:CHAN, 0:NLAT] = own_ref[...]
    for h in range(2):
        piece = jnp.transpose(square_ref[:, 128 * h : 128 * h + 128])
        piece = jnp.where(lanes_of((128, 128)) < CHAN, piece, 0.0)
        height = 128 if h == 0 else NLAT - 128
        gain_ref[128 * h : 128 * h + height, :] = (piece + turn(piece, 32))[:height, :]
    copies.append(begin(gain_ref, gain_out, sems.at[5]))
    weight = sine[0:1, :] * (math.pi / NLAT)
    blank = jnp.zeros((128 - NLAT // 2, 128), F32)
    for m in range(8):
        for parity in range(2):
            p = jnp.where(lanes_of((96, 128)) < 96, table[pl.ds(8 * parity + m, 96, stride=16), :], 0.0)
            p_ref[m, 96 * parity : 96 * parity + 96, :] = (p * weight).astype(BF)
            turned = jnp.transpose(jnp.concatenate([p, blank], axis=0))
            pt_ref[m, 96 * parity : 96 * parity + 96, :] = turned[:96, :].astype(BF)
        if m % 4 == 3:
            at = pl.ds(m - 3, 4)
            copies.append(begin(p_ref.at[at], p_out.at[at], sems.at[m // 4]))
            copies.append(begin(pt_ref.at[at], pt_out.at[at], sems.at[2 + m // 4]))
    for copy in copies:
        copy.wait()


def spectrum_body(recv_ref, fhi_ref, flo_ref, unused_a, unused_b, send_out, full_out, wide, full_ref, send_ref, sems):
    wide[...] = recv_ref[...].astype(F32).reshape(LON * 16, 128)
    shape = (LON, 128)
    for e in range(2):
        for h in range(2):
            total = [jnp.zeros(shape, F32)] * PAIRS
            for s in range(4):
                rows = wide[pl.ds(8 * e + 4 * h + s, LON, stride=16), :]
                for q in range(PAIRS):
                    total[q] = jnp.where(inside(shape, 32 * s, CHAN), turn(rows, 32 * s - CHAN * q), total[q])
            for q in range(PAIRS):
                kap = 2 * q + e
                full_ref[32 * kap : 32 * kap + 32, 128 * h : 128 * h + 128] = total[q].astype(BF)
    copies = [begin(full_ref, full_out, sems.at[1])]
    full = full_ref[...]
    spectrum = jnp.dot(fhi_ref[...], full, preferred_element_type=F32)
    spectrum = spectrum + jnp.dot(flo_ref[...], full, preferred_element_type=F32)
    send_ref[...] = spectrum.astype(BF).reshape(LAT, 16, 256)
    copies.append(begin(send_ref, send_out, sems.at[0]))
    for copy in copies:
        copy.wait()


def row_after(x):
    slot = lax.broadcasted_iota(jnp.int32, x.shape, 0)
    half = LAT // 2
    moved = jnp.where(slot < half - 1, pltpu.roll(x, LAT - 1, 0), pltpu.roll(x, 1, 0))
    return jnp.where(slot == half - 1, swap_halves(x), jnp.where(slot == half, 0.0, moved))


def row_before(x):
    slot = lax.broadcasted_iota(jnp.int32, x.shape, 0)
    half = LAT // 2
    moved = jnp.where(slot < half, pltpu.roll(x, 1, 0), pltpu.roll(x, LAT - 1, 0))
    return jnp.where(slot == LAT - 1, swap_halves(x), jnp.where(slot == 0, 0.0, moved))


def filter_body(
    band_ref, recv_ref, p_in, pt_in, gain_in, taps_ref, send_out, wide, out, p_ref, pt_ref, gain_ref, send_ref, sems
):
    cuts = [pl.ds(4 * i, 4) for i in range(2)]
    tables = []
    for i, at in enumerate(cuts):
        tables.append([begin(p_in.at[at], p_ref.at[at], sems.at[2 * i])])
        if i == 0:
            tables[0].append(begin(gain_in, gain_ref, sems.at[4]))
        tables[i].append(begin(pt_in.at[at], pt_ref.at[at], sems.at[2 * i + 1]))
    rows = LAT * 16
    for h in range(2):
        wide[rows * h : rows * h + rows, :] = recv_ref[:, :, 128 * h : 128 * h + 128].astype(F32).reshape(rows, 128)
    shape = (LAT, 128)
    lane = lanes_of(shape)
    blank = jnp.zeros((32, 128), F32)
    order = lax.broadcasted_iota(jnp.int32, (8, 128), 0) + band_ref[0] * 8
    second = ((lanes_of((8, 128)) >> 5) & 1) == 1
    highest = (order == 0) & second
    turn_cosine = jnp.where(highest, -1.0, wave(order, 0, 1)) * (0.5 / math.pi)
    turn_sine = jnp.where(second, -1.0, 1.0) * wave(order, 1, 1) * (0.5 / math.pi)
    used = jnp.where(highest, 0.0, 1.0)
    taps = [taps_ref[i : i + 1, 0:128] for i in range(9)]
    for m in range(8):
        chunks, partners = [], []
        for h in range(2):
            low, high = (wide[pl.ds(rows * h + 8 * p + m, LAT, stride=16), :] for p in range(2))
            for s in range(4):
                chunks.append(jnp.where(lane < 32, turn(low, -32 * s), turn(high, 32 - 32 * s)))
                partners.append(jnp.where(lane < 32, turn(high, -32 * s), turn(low, 32 - 32 * s)))
        mixed = []
        for i in range(3):
            west, here, east = taps[3 * i : 3 * i + 3]
            along = here * (0.5 / math.pi) + (west + east) * turn_cosine[m : m + 1, :]
            across = (east - west) * turn_sine[m : m + 1, :]
            mixed.append([along * chunks[r] + across * partners[r] for r in range(8)])
        above = [row_before(mixed[0][7])] + mixed[0][:7]
        below = mixed[2][1:] + [row_after(mixed[2][0])]
        local = [above[r] + mixed[1][r] + below[r] for r in range(8)]
        if m == 0:
            chunks = [chunk * used[0:1, :] for chunk in chunks]
        mirrored = [swap_halves(chunks[7 - r]) for r in range(4)]
        even = jnp.concatenate([chunks[r] + mirrored[r] for r in range(4)] + [blank], axis=0).astype(BF)
        odd = jnp.concatenate([chunks[r] - mirrored[r] for r in range(4)] + [blank], axis=0).astype(BF)
        if m % 4 == 0:
            for copy in tables[m // 4]:
                copy.wait()
        halves_back = []
        for parity in range(2):
            at = slice(96 * parity, 96 * parity + 96)
            field = even if (parity + m) % 2 == 0 else odd
            scaled = jnp.dot(p_ref[m, at, :], field, preferred_element_type=F32)
            scaled = scaled * gain_ref[pl.ds(parity, 96, stride=2), :]
            scaled = jnp.concatenate([scaled, blank], axis=0).astype(BF)
            halves_back.append(jnp.dot(pt_ref[m, at, :], scaled, preferred_element_type=F32))
        if m % 2 == 1:
            halves_back.reverse()
        near, far = halves_back[0] + halves_back[1], halves_back[0] - halves_back[1]
        back = [near[LAT * r : LAT * r + LAT, :] for r in range(4)]
        back = back + [swap_halves(far[LAT * r : LAT * r + LAT, :]) for r in (3, 2, 1, 0)]
        back = [back[r] + local[r] for r in range(8)]
        for p in range(2):
            for h in range(2):
                total = jnp.zeros(shape, F32)
                for s in range(4):
                    r = 4 * h + s
                    total = jnp.where(
                        inside(shape, 32 * s, 32), turn(back[r], 32 * s - 32 * p), total
                    )
                out[pl.ds(rows * h + 8 * p + m, LAT, stride=16), :] = total
    for h in range(2):
        send_ref[:, :, 128 * h : 128 * h + 128] = out[rows * h : rows * h + rows, :].astype(BF).reshape(LAT, 16, 128)
    begin(send_ref, send_out, sems.at[5]).wait()


def synthesis_body(recv_ref, base_in, send_out, inv_ref, base_ref, send_ref, out, summed_ref, sems):
    base = begin(base_in, base_ref, sems.at[0])
    shape = (LON, NLON)
    order, part = mode_of(lanes_of(shape))
    column = COLS * lax.broadcasted_iota(jnp.int32, shape, 0)
    weight = jnp.where((order == 0) | (order == NLON // 2), 1.0, 2.0)
    cosine, sine = wave(order, part, column) * weight, wave(order, part + 1, column) * weight
    shape = (16, NLON)
    order, _ = mode_of(lanes_of(shape))
    column = lax.broadcasted_iota(jnp.int32, shape, 0)
    step_cosine, step_sine = wave(order, 0, column), wave(order, 1, column)
    for kap in range(COLS):
        turned = cosine * step_cosine[kap : kap + 1, :] - sine * step_sine[kap : kap + 1, :]
        inv_ref[32 * kap : 32 * kap + 32, :] = turned.astype(BF)
    summed_ref[...] = jnp.dot(inv_ref[...], recv_ref[...].reshape(NLON, 256), preferred_element_type=F32)
    base.wait()
    summed_ref[...] += base_ref[...].astype(F32)
    shape = (LON, 128)
    for e in range(2):
        for h in range(2):
            for s in range(4):
                total = jnp.zeros(shape, F32)
                for q in range(PAIRS):
                    kap = 2 * q + e
                    rows = summed_ref[32 * kap : 32 * kap + 32, 128 * h : 128 * h + 128]
                    total = jnp.where(inside(shape, CHAN * q, CHAN), turn(rows, CHAN * q - 32 * s), total)
                out[pl.ds(8 * e + 4 * h + s, LON, stride=16), :] = total
    send_ref[...] = out[...].astype(BF).reshape(LON, 16, 128)
    begin(send_ref, send_out, sems.at[1]).wait()


def mlp_body(recv_ref, gain_ref, win_ref, wout_ref, out_ref, summed_ref):
    shape = (16, 128)
    lane = lanes_of(shape)
    for tile in range(5):
        for q in range(PAIRS):
            total = jnp.zeros(shape, F32)
            for d in range(128 * tile // CHAN, (128 * tile + 127) // CHAN + 1):
                off = CHAN * d - 128 * tile
                piece = turn(recv_ref[d].astype(F32), off - CHAN * q)
                total = jnp.where((lane >= off) & (lane < off + CHAN), piece, total)
            summed_ref[16 * q : 16 * q + 16, 128 * tile : 128 * tile + 128] = total
    summed = summed_ref[...]
    mean = jnp.sum(summed * summed, axis=1, keepdims=True) * (1.0 / summed.shape[1])
    normed = (summed * lax.rsqrt(mean + EPS) * gain_ref[...]).astype(BF)
    hidden = jnp.dot(normed, win_ref[...], preferred_element_type=F32)
    hidden = (0.5 * hidden * (1.0 + lax.erf(hidden * math.sqrt(0.5)))).astype(BF)
    result = summed + jnp.dot(hidden, wout_ref[...], preferred_element_type=F32)
    out_ref[...] = result.astype(BF)


def on_device(latent_field, spectral_filter, conv_weight, norm_gain, weight_in, weight_out):
    channels = latent_field.shape[0]
    points = COLS * ROWS
    table, circle, group, mode = (NLON, NLON), (NLON, 256), (LON, 16, 128), (LAT, 16, 256)
    field = jnp.transpose(latent_field, (2, 1, 0)).reshape(points, channels)
    pieces = call(
        pack_body,
        [(group, BF, HBM)],
        [(field, HBM)],
        [VMEM((points, channels), BF), VMEM(group, BF), pltpu.SemaphoreType.DMA((5,))],
        name="pack",
    )
    pieces = lax.all_to_all(pieces, "lon", 0, 0, tiled=True)

    sector = lax.axis_index("lon").astype(jnp.int32).reshape(1)
    band = lax.axis_index("lat").astype(jnp.int32).reshape(1)
    fhi, flo, taps = call(
        fourier_body,
        [(table, BF, VMEM), (table, BF, VMEM), ((16, 256), F32, VMEM)],
        [(sector, SMEM), (conv_weight, HBM)],
        [VMEM(conv_weight.shape, F32), pltpu.SemaphoreType.DMA],
        name="fourier_tables",
        flops=10_000_000,
    )
    polynomials = (8, NLAT, 128)
    p, pt, gain = call(
        legendre_body,
        [(polynomials, BF, HBM), (polynomials, BF, HBM), ((NLAT, 128), F32, HBM)],
        [(band, SMEM), (spectral_filter, HBM)],
        [VMEM((NLAT * 8, 128), F32), VMEM(polynomials, BF), VMEM(polynomials, BF)]
        + [VMEM((NLAT, 128), F32), VMEM((CHAN, NLAT), F32), VMEM((128, 256), F32), pltpu.SemaphoreType.DMA((6,))],
        name="legendre_tables",
        flops=10_000_000,
    )
    norm_gain = norm_gain.reshape(1, channels)
    modes, full = call(
        spectrum_body,
        [(mode, BF, HBM), (circle, BF, HBM)],
        [(pieces, VMEM), (fhi, VMEM), (flo, VMEM), (gain, HBM), (norm_gain, HBM)],
        [VMEM((LON * 16, 128), F32), VMEM(circle, BF), VMEM(mode, BF), pltpu.SemaphoreType.DMA((2,))],
        name="spectrum",
    )
    modes = lax.all_to_all(modes, "lat", 0, 0, tiled=True, axis_index_groups=[SLOTS])
    modes = call(
        filter_body,
        [(mode, BF, HBM)],
        [(band, SMEM), (modes, VMEM), (p, HBM), (pt, HBM), (gain, HBM), (taps, VMEM)],
        [VMEM((2 * LAT * 16, 128), F32)] * 2
        + [VMEM(polynomials, BF)] * 2
        + [VMEM((NLAT, 128), F32), VMEM(mode, BF), pltpu.SemaphoreType.DMA((6,))],
        name="filter",
    )
    modes = lax.all_to_all(modes, "lat", 0, 0, tiled=True, axis_index_groups=[SLOTS])
    pieces = call(
        synthesis_body,
        [(group, BF, HBM)],
        [(modes, VMEM), (full, HBM)],
        [VMEM(table, BF), VMEM(circle, BF), VMEM(group, BF), VMEM((LON * 16, 128), F32), VMEM(circle, F32)]
        + [pltpu.SemaphoreType.DMA((2,))],
        name="synthesis",
    )
    pieces = lax.all_to_all(pieces, "lon", 0, 0, tiled=True)
    result = call(
        mlp_body,
        [((points, channels), BF, VMEM)],
        [(pieces, VMEM), (norm_gain, VMEM), (weight_in, VMEM), (weight_out, VMEM)],
        [VMEM((points, channels), F32)],
        name="mlp",
    )
    return jnp.transpose(result.reshape(COLS, ROWS, channels), (2, 1, 0))


def solution(mesh):
    in_specs = (P(None, "lat", "lon"), P("lon", None), P(), P(), P(), P())
    return jax.shard_map(on_device, mesh=mesh, in_specs=in_specs, out_specs=P(None, "lat", "lon"), check_vma=False)
```

```python
import math

import jax
import jax.numpy as jnp
from jax import lax
from jax.experimental import pallas as pl
from jax.experimental.pallas import tpu as pltpu
from jax.sharding import PartitionSpec as P

LON, LAT, COLS, ROWS, CHAN = 32, 24, 12, 8, 20
NLON, NLAT = LON * COLS, LAT * ROWS
PAIRS = COLS // 2
BF, F32 = jnp.bfloat16, jnp.float32
EPS = 1e-06
SLOTS = [*range(LAT // 2), *range(LAT - 1, LAT // 2 - 1, -1)]


def lanes_of(shape):
    return lax.broadcasted_iota(jnp.int32, shape, 1)


def inside(shape, start, width):
    lane = lanes_of(shape)
    return (lane >= start) & (lane < start + width)


def turn(x, shift):
    shift %= 128
    return x if shift == 0 else pltpu.roll(x, shift, 1)


VMEM, HBM, ANY, SMEM = pltpu.VMEM, pltpu.HBM, pl.ANY, pltpu.SMEM


def call(body, outs, args, scratch=(), name=None, mib=24, flops=0):
    result = pl.pallas_call(
        body,
        out_shape=[
            HBM(shape, kind) if space is HBM else jax.ShapeDtypeStruct(shape, kind) for shape, kind, space in outs
        ],
        in_specs=[pl.BlockSpec(memory_space=space) for _, space in args],
        out_specs=[pl.BlockSpec(memory_space=space) for _, _, space in outs],
        scratch_shapes=list(scratch),
        compiler_params=pltpu.CompilerParams(vmem_limit_bytes=mib * 2**20),
        cost_estimate=pl.CostEstimate(flops=flops, bytes_accessed=1_000_000, transcendentals=0),
        name=name,
    )(*(pltpu.with_memory_space_constraint(array, HBM) if space is HBM else array for array, space in args))
    return result[0] if len(outs) == 1 else result


def swap_halves(x):
    return pltpu.roll(x, LAT // 2, 0)


def begin(source, target, sem):
    copy = pltpu.make_async_copy(source, target, sem)
    copy.start()
    return copy


def pack_body(field_ref, out_ref, x_ref, send_ref, sems):
    shape = (16, 128)
    begin(field_ref, x_ref, sems.at[4]).wait()
    copies = []
    for d in range(LON):
        tile, off = divmod(CHAN * d, 128)
        last = (CHAN * d + CHAN - 1) // 128
        total = jnp.zeros(shape, F32)
        for q in range(PAIRS):
            at = slice(16 * q, 16 * q + 16)
            piece = x_ref[at, 128 * tile : 128 * tile + 128].astype(F32)
            if last > tile:
                after = x_ref[at, 128 * last : 128 * last + 128].astype(F32)
                piece = jnp.where(lanes_of(shape) >= off, piece, after)
            total = jnp.where(inside(shape, CHAN * q, CHAN), turn(piece, CHAN * q - off), total)
        send_ref[d] = total.astype(BF)
        if d % 8 == 7:
            at = pl.ds(d - 7, 8)
            copies.append(begin(send_ref.at[at], out_ref.at[at], sems.at[d // 8]))
    for copy in copies:
        copy.wait()


def wave(order, part, column):
    v = (order * column + part * (NLON // 4)).astype(F32)
    index = v - NLON * jnp.floor(v * (1.0 / NLON))
    x = (NLON // 4 - jnp.abs(index - NLON // 2)) * (2.0 * math.pi / NLON)
    y = x * x
    s = 1.0 / 6227020800.0
    for term in (-1.0 / 39916800.0, 1.0 / 362880.0, -1.0 / 5040.0, 1.0 / 120.0, -1.0 / 6.0, 1.0):
        s = s * y + term
    return -(s * x)


def mode_of(n):
    slot = n >> 4
    device = jnp.where(slot < LAT // 2, slot, LAT + LAT // 2 - 1 - slot)
    order, part = (device << 3) + (n & 7), (n >> 3) & 1
    highest = (order == 0) & (part == 1)
    return jnp.where(highest, NLON // 2, order), jnp.where(highest, 0, part)


def column_of(k):
    return COLS * (k & 31) + (k >> 5)


def halves(x):
    high = x.astype(BF)
    return high, (x - high.astype(F32)).astype(BF)


def fourier_body(sector_ref, kernel_in, fhi_ref, flo_ref, taps_ref, kernel_ref, sem):
    arriving = begin(kernel_in, kernel_ref, sem)
    shape = (16, NLON)
    lane = lanes_of(shape)

    def block(b, unused):
        row = lax.broadcasted_iota(jnp.int32, shape, 0) + 16 * b
        at = pl.ds(pl.multiple_of(16 * b, 16), 16)
        order, part = mode_of(row)
        table = wave(order, part, column_of(lane)) * (2.0 * math.pi / NLON)
        fhi_ref[at, :], flo_ref[at, :] = halves(table)
        return unused

    lax.fori_loop(0, NLON // 16, block, 0)
    arriving.wait()
    wide = (kernel_ref.shape[1], 256)
    own = lanes_of(wide) & 31
    channel = lax.broadcasted_iota(jnp.int32, wide, 0)
    picked = (channel == own + sector_ref[0] * CHAN) & (own < CHAN)
    taps_ref[0:9, :] = jnp.dot(
        kernel_ref[...], jnp.where(picked, 1.0, 0.0), precision=lax.Precision.HIGHEST, preferred_element_type=F32
    )


def legendre_body(band_ref, gain_in, p_ref, pt_ref, gain_ref, table, own_ref, square_ref, sem):
    arriving = begin(gain_in, own_ref, sem)
    shape = (8, 128)
    lane = lanes_of(shape)
    order_i = lax.broadcasted_iota(jnp.int32, shape, 0) + band_ref[0] * 8
    order = order_i.astype(F32)
    r = jnp.floor((lane.astype(F32) + 0.5) * (1.0 / LAT))
    slot = lane.astype(F32) - LAT * r
    device = jnp.where(slot < LAT // 2, slot, LAT + LAT // 2 - 1.0 - slot)
    row = jnp.minimum(8.0 * device + r, NLAT - 1.0)
    theta = (row + 0.5) * (math.pi / NLAT)
    cosine, sine = jnp.cos(theta), jnp.sin(theta)
    k = lanes_of((8, 256)).astype(F32) + 1.0
    ratio = jnp.log((2.0 * k - 1.0) / (2.0 * k))
    factor = jnp.sum(jnp.where(k <= order[:, 0:1], ratio, 0.0), axis=1, keepdims=True)
    start = 0.5 * jnp.log((2.0 * order + 1.0) / (4.0 * math.pi)) + 0.5 * factor + order * jnp.log(sine)
    square = order * order
    every = 16

    def block(b, carry):
        before, current, log_scale = carry
        scale = jnp.exp(log_scale)
        for t in range(every):
            degree = b * every + t
            l = degree.astype(F32)
            lower = (l - 1.0) * (l - 1.0)
            alpha = jnp.sqrt((4.0 * l * l - 1.0) / jnp.maximum(l * l - square, 1.0))
            beta = jnp.sqrt(jnp.maximum(lower - square, 0.0) / jnp.maximum(4.0 * lower - 1.0, 1.0))
            fresh = (alpha * cosine) * current - (alpha * beta) * before
            fresh = jnp.where(order_i == degree, 1.0, fresh)
            fresh = jnp.where(order_i > degree, 0.0, fresh)
            before, current = current, fresh
            table[pl.ds(pl.multiple_of(degree * 8, 8), 8), :] = fresh * scale
        largest = jnp.maximum(jnp.abs(before), jnp.abs(current))
        largest = jnp.where(order_i <= b * every + (every - 1), largest, 1.0)
        return before / largest, current / largest, log_scale + jnp.log(largest)

    blank = jnp.zeros(shape, F32)
    lax.fori_loop(0, NLAT // every, block, (blank, blank, start))
    arriving.wait()
    square_ref[0:CHAN, 0:NLAT] = own_ref[...]
    for h in range(2):
        piece = jnp.transpose(square_ref[:, 128 * h : 128 * h + 128])
        piece = jnp.where(lanes_of((128, 128)) < CHAN, piece, 0.0)
        height = 128 if h == 0 else NLAT - 128
        gain_ref[128 * h : 128 * h + height, :] = (piece + turn(piece, 32))[:height, :]
    weight = sine[0:1, :] * (math.pi / NLAT)
    blank = jnp.zeros((128 - NLAT // 2, 128), F32)
    for m in range(8):
        for parity in range(2):
            p = jnp.where(lanes_of((96, 128)) < 96, table[pl.ds(8 * parity + m, 96, stride=16), :], 0.0)
            p_ref[m, 96 * parity : 96 * parity + 96, :] = (p * weight).astype(BF)
            turned = jnp.transpose(jnp.concatenate([p, blank], axis=0))
            pt_ref[m, 96 * parity : 96 * parity + 96, :] = turned[:96, :].astype(BF)


def spectrum_body(recv_ref, fhi_ref, flo_ref, unused_a, unused_b, send_out, full_ref, wide, send_ref, sem):
    wide[...] = recv_ref[...].astype(F32).reshape(LON * 16, 128)
    shape = (LON, 128)
    for e in range(2):
        for h in range(2):
            total = [jnp.zeros(shape, F32)] * PAIRS
            for s in range(4):
                rows = wide[pl.ds(8 * e + 4 * h + s, LON, stride=16), :]
                for q in range(PAIRS):
                    total[q] = jnp.where(inside(shape, 32 * s, CHAN), turn(rows, 32 * s - CHAN * q), total[q])
            for q in range(PAIRS):
                kap = 2 * q + e
                full_ref[32 * kap : 32 * kap + 32, 128 * h : 128 * h + 128] = total[q].astype(BF)
    full = full_ref[...]
    spectrum = jnp.dot(fhi_ref[...], full, preferred_element_type=F32)
    spectrum = spectrum + jnp.dot(flo_ref[...], full, preferred_element_type=F32)
    send_ref[...] = spectrum.astype(BF).reshape(LAT, 16, 256)
    begin(send_ref, send_out, sem).wait()


def row_after(x):
    slot = lax.broadcasted_iota(jnp.int32, x.shape, 0)
    half = LAT // 2
    moved = jnp.where(slot < half - 1, pltpu.roll(x, LAT - 1, 0), pltpu.roll(x, 1, 0))
    return jnp.where(slot == half - 1, swap_halves(x), jnp.where(slot == half, 0.0, moved))


def row_before(x):
    slot = lax.broadcasted_iota(jnp.int32, x.shape, 0)
    half = LAT // 2
    moved = jnp.where(slot < half, pltpu.roll(x, 1, 0), pltpu.roll(x, LAT - 1, 0))
    return jnp.where(slot == LAT - 1, swap_halves(x), jnp.where(slot == 0, 0.0, moved))


def filter_body(
    band_ref, recv_ref, p_ref, pt_ref, gain_ref, taps_ref, send_out, wide, out, send_ref, sem
):
    rows = LAT * 16
    for h in range(2):
        wide[rows * h : rows * h + rows, :] = recv_ref[:, :, 128 * h : 128 * h + 128].astype(F32).reshape(rows, 128)
    shape = (LAT, 128)
    lane = lanes_of(shape)
    blank = jnp.zeros((32, 128), F32)
    order = lax.broadcasted_iota(jnp.int32, (8, 128), 0) + band_ref[0] * 8
    second = ((lanes_of((8, 128)) >> 5) & 1) == 1
    highest = (order == 0) & second
    turn_cosine = jnp.where(highest, -1.0, wave(order, 0, 1)) * (0.5 / math.pi)
    turn_sine = jnp.where(second, -1.0, 1.0) * wave(order, 1, 1) * (0.5 / math.pi)
    used = jnp.where(highest, 0.0, 1.0)
    taps = [taps_ref[i : i + 1, 0:128] for i in range(9)]
    for m in range(8):
        chunks, partners = [], []
        for h in range(2):
            low, high = (wide[pl.ds(rows * h + 8 * p + m, LAT, stride=16), :] for p in range(2))
            for s in range(4):
                chunks.append(jnp.where(lane < 32, turn(low, -32 * s), turn(high, 32 - 32 * s)))
                partners.append(jnp.where(lane < 32, turn(high, -32 * s), turn(low, 32 - 32 * s)))
        mixed = []
        for i in range(3):
            west, here, east = taps[3 * i : 3 * i + 3]
            along = here * (0.5 / math.pi) + (west + east) * turn_cosine[m : m + 1, :]
            across = (east - west) * turn_sine[m : m + 1, :]
            mixed.append([along * chunks[r] + across * partners[r] for r in range(8)])
        above = [row_before(mixed[0][7])] + mixed[0][:7]
        below = mixed[2][1:] + [row_after(mixed[2][0])]
        local = [above[r] + mixed[1][r] + below[r] for r in range(8)]
        if m == 0:
            chunks = [chunk * used[0:1, :] for chunk in chunks]
        mirrored = [swap_halves(chunks[7 - r]) for r in range(4)]
        even = jnp.concatenate([chunks[r] + mirrored[r] for r in range(4)] + [blank], axis=0).astype(BF)
        odd = jnp.concatenate([chunks[r] - mirrored[r] for r in range(4)] + [blank], axis=0).astype(BF)
        halves_back = []
        for parity in range(2):
            at = slice(96 * parity, 96 * parity + 96)
            field = even if (parity + m) % 2 == 0 else odd
            scaled = jnp.dot(p_ref[m, at, :], field, preferred_element_type=F32)
            scaled = scaled * gain_ref[pl.ds(parity, 96, stride=2), :]
            scaled = jnp.concatenate([scaled, blank], axis=0).astype(BF)
            halves_back.append(jnp.dot(pt_ref[m, at, :], scaled, preferred_element_type=F32))
        if m % 2 == 1:
            halves_back.reverse()
        near, far = halves_back[0] + halves_back[1], halves_back[0] - halves_back[1]
        back = [near[LAT * r : LAT * r + LAT, :] for r in range(4)]
        back = back + [swap_halves(far[LAT * r : LAT * r + LAT, :]) for r in (3, 2, 1, 0)]
        back = [back[r] + local[r] for r in range(8)]
        for p in range(2):
            for h in range(2):
                total = jnp.zeros(shape, F32)
                for s in range(4):
                    r = 4 * h + s
                    total = jnp.where(
                        inside(shape, 32 * s, 32), turn(back[r], 32 * s - 32 * p), total
                    )
                out[pl.ds(rows * h + 8 * p + m, LAT, stride=16), :] = total
    for h in range(2):
        send_ref[:, :, 128 * h : 128 * h + 128] = out[rows * h : rows * h + rows, :].astype(BF).reshape(LAT, 16, 128)
    begin(send_ref, send_out, sem).wait()


def synthesis_body(recv_ref, base_ref, send_out, inv_ref, send_ref, out, summed_ref, sem):
    shape = (LON, NLON)
    order, part = mode_of(lanes_of(shape))
    column = COLS * lax.broadcasted_iota(jnp.int32, shape, 0)
    weight = jnp.where((order == 0) | (order == NLON // 2), 1.0, 2.0)
    cosine, sine = wave(order, part, column) * weight, wave(order, part + 1, column) * weight
    shape = (16, NLON)
    order, _ = mode_of(lanes_of(shape))
    column = lax.broadcasted_iota(jnp.int32, shape, 0)
    step_cosine, step_sine = wave(order, 0, column), wave(order, 1, column)
    for kap in range(COLS):
        turned = cosine * step_cosine[kap : kap + 1, :] - sine * step_sine[kap : kap + 1, :]
        inv_ref[32 * kap : 32 * kap + 32, :] = turned.astype(BF)
    summed_ref[...] = jnp.dot(inv_ref[...], recv_ref[...].reshape(NLON, 256), preferred_element_type=F32)
    summed_ref[...] += base_ref[...].astype(F32)
    shape = (LON, 128)
    for e in range(2):
        for h in range(2):
            for s in range(4):
                total = jnp.zeros(shape, F32)
                for q in range(PAIRS):
                    kap = 2 * q + e
                    rows = summed_ref[32 * kap : 32 * kap + 32, 128 * h : 128 * h + 128]
                    total = jnp.where(inside(shape, CHAN * q, CHAN), turn(rows, CHAN * q - 32 * s), total)
                out[pl.ds(8 * e + 4 * h + s, LON, stride=16), :] = total
    send_ref[...] = out[...].astype(BF).reshape(LON, 16, 128)
    begin(send_ref, send_out, sem).wait()


def mlp_body(recv_ref, gain_ref, win_ref, wout_ref, out_ref, summed_ref):
    shape = (16, 128)
    lane = lanes_of(shape)
    for tile in range(5):
        for q in range(PAIRS):
            total = jnp.zeros(shape, F32)
            for d in range(128 * tile // CHAN, (128 * tile + 127) // CHAN + 1):
                off = CHAN * d - 128 * tile
                piece = turn(recv_ref[d].astype(F32), off - CHAN * q)
                total = jnp.where((lane >= off) & (lane < off + CHAN), piece, total)
            summed_ref[16 * q : 16 * q + 16, 128 * tile : 128 * tile + 128] = total
    summed = summed_ref[...]
    mean = jnp.sum(summed * summed, axis=1, keepdims=True) * (1.0 / summed.shape[1])
    normed = (summed * lax.rsqrt(mean + EPS) * gain_ref[...]).astype(BF)
    hidden = jnp.dot(normed, win_ref[...], preferred_element_type=F32)
    hidden = (0.5 * hidden * (1.0 + lax.erf(hidden * math.sqrt(0.5)))).astype(BF)
    result = summed + jnp.dot(hidden, wout_ref[...], preferred_element_type=F32)
    out_ref[...] = result.astype(BF)


def on_device(latent_field, spectral_filter, conv_weight, norm_gain, weight_in, weight_out):
    channels = latent_field.shape[0]
    points = COLS * ROWS
    table, circle, group, mode = (NLON, NLON), (NLON, 256), (LON, 16, 128), (LAT, 16, 256)
    field = jnp.transpose(latent_field, (2, 1, 0)).reshape(points, channels)
    pieces = call(
        pack_body,
        [(group, BF, HBM)],
        [(field, HBM)],
        [VMEM((points, channels), BF), VMEM(group, BF), pltpu.SemaphoreType.DMA((5,))],
        name="pack",
    )
    pieces = lax.all_to_all(pieces, "lon", 0, 0, tiled=True)

    sector = lax.axis_index("lon").astype(jnp.int32).reshape(1)
    band = lax.axis_index("lat").astype(jnp.int32).reshape(1)
    fhi, flo, taps = call(
        fourier_body,
        [(table, BF, VMEM), (table, BF, VMEM), ((16, 256), F32, VMEM)],
        [(sector, SMEM), (conv_weight, HBM)],
        [VMEM(conv_weight.shape, F32), pltpu.SemaphoreType.DMA],
        name="fourier_tables",
        flops=10_000_000,
    )
    polynomials = (8, NLAT, 128)
    p, pt, gain = call(
        legendre_body,
        [(polynomials, BF, VMEM), (polynomials, BF, VMEM), ((NLAT, 128), F32, VMEM)],
        [(band, SMEM), (spectral_filter, HBM)],
        [VMEM((NLAT * 8, 128), F32), VMEM((CHAN, NLAT), F32), VMEM((128, 256), F32), pltpu.SemaphoreType.DMA],
        name="legendre_tables",
        flops=10_000_000,
    )
    norm_gain = norm_gain.reshape(1, channels)
    modes, full = call(
        spectrum_body,
        [(mode, BF, HBM), (circle, BF, VMEM)],
        [(pieces, VMEM), (fhi, VMEM), (flo, VMEM), (gain, VMEM), (norm_gain, HBM)],
        [VMEM((LON * 16, 128), F32), VMEM(mode, BF), pltpu.SemaphoreType.DMA],
        name="spectrum",
    )
    modes = lax.all_to_all(modes, "lat", 0, 0, tiled=True, axis_index_groups=[SLOTS])
    modes = call(
        filter_body,
        [(mode, BF, HBM)],
        [(band, SMEM), (modes, VMEM), (p, VMEM), (pt, VMEM), (gain, VMEM), (taps, VMEM)],
        [VMEM((2 * LAT * 16, 128), F32)] * 2 + [VMEM(mode, BF), pltpu.SemaphoreType.DMA],
        name="filter",
    )
    modes = lax.all_to_all(modes, "lat", 0, 0, tiled=True, axis_index_groups=[SLOTS])
    pieces = call(
        synthesis_body,
        [(group, BF, HBM)],
        [(modes, VMEM), (full, VMEM)],
        [VMEM(table, BF), VMEM(group, BF), VMEM((LON * 16, 128), F32), VMEM(circle, F32), pltpu.SemaphoreType.DMA],
        name="synthesis",
    )
    pieces = lax.all_to_all(pieces, "lon", 0, 0, tiled=True)
    result = call(
        mlp_body,
        [((points, channels), BF, VMEM)],
        [(pieces, VMEM), (norm_gain, VMEM), (weight_in, VMEM), (weight_out, VMEM)],
        [VMEM((points, channels), F32)],
        name="mlp",
    )
    return jnp.transpose(result.reshape(COLS, ROWS, channels), (2, 1, 0))


def solution(mesh):
    in_specs = (P(None, "lat", "lon"), P("lon", None), P(), P(), P(), P())
    return jax.shard_map(on_device, mesh=mesh, in_specs=in_specs, out_specs=P(None, "lat", "lon"), check_vma=False)
```

```python
import math

import jax
import jax.numpy as jnp
from jax import lax
from jax.experimental import pallas as pl
from jax.experimental.pallas import tpu as pltpu
from jax.sharding import PartitionSpec as P

LON, LAT, COLS, ROWS, CHAN = 32, 24, 12, 8, 20
NLON, NLAT = LON * COLS, LAT * ROWS
PAIRS = COLS // 2
BF, F32 = jnp.bfloat16, jnp.float32
EPS = 1e-06
SLOTS = [*range(LAT // 2), *range(LAT - 1, LAT // 2 - 1, -1)]


def lanes_of(shape):
    return lax.broadcasted_iota(jnp.int32, shape, 1)


def inside(shape, start, width):
    lane = lanes_of(shape)
    return (lane >= start) & (lane < start + width)


def turn(x, shift):
    shift %= 128
    return x if shift == 0 else pltpu.roll(x, shift, 1)


VMEM, HBM, ANY, SMEM = pltpu.VMEM, pltpu.HBM, pl.ANY, pltpu.SMEM


def call(body, outs, args, scratch=(), name=None, mib=24, flops=0):
    result = pl.pallas_call(
        body,
        out_shape=[
            HBM(shape, kind) if space is HBM else jax.ShapeDtypeStruct(shape, kind) for shape, kind, space in outs
        ],
        in_specs=[pl.BlockSpec(memory_space=space) for _, space in args],
        out_specs=[pl.BlockSpec(memory_space=space) for _, _, space in outs],
        scratch_shapes=list(scratch),
        compiler_params=pltpu.CompilerParams(vmem_limit_bytes=mib * 2**20),
        cost_estimate=pl.CostEstimate(flops=flops, bytes_accessed=1_000_000, transcendentals=0),
        name=name,
    )(*(pltpu.with_memory_space_constraint(array, HBM) if space is HBM else array for array, space in args))
    return result[0] if len(outs) == 1 else result


def swap_halves(x):
    return pltpu.roll(x, LAT // 2, 0)


def begin(source, target, sem):
    copy = pltpu.make_async_copy(source, target, sem)
    copy.start()
    return copy


def pack_body(field_ref, out_ref, x_ref, send_ref, sems):
    shape = (16, 128)
    begin(field_ref, x_ref, sems.at[4]).wait()
    copies = []
    for d in range(LON):
        tile, off = divmod(CHAN * d, 128)
        last = (CHAN * d + CHAN - 1) // 128
        total = jnp.zeros(shape, F32)
        for q in range(PAIRS):
            at = slice(16 * q, 16 * q + 16)
            piece = x_ref[at, 128 * tile : 128 * tile + 128].astype(F32)
            if last > tile:
                after = x_ref[at, 128 * last : 128 * last + 128].astype(F32)
                piece = jnp.where(lanes_of(shape) >= off, piece, after)
            total = jnp.where(inside(shape, CHAN * q, CHAN), turn(piece, CHAN * q - off), total)
        send_ref[d] = total.astype(BF)
        if d % 8 == 7:
            at = pl.ds(d - 7, 8)
            copies.append(begin(send_ref.at[at], out_ref.at[at], sems.at[d // 8]))
    for copy in copies:
        copy.wait()


def wave(order, part, column):
    v = (order * column + part * (NLON // 4)).astype(F32)
    index = v - NLON * jnp.floor(v * (1.0 / NLON))
    x = (NLON // 4 - jnp.abs(index - NLON // 2)) * (2.0 * math.pi / NLON)
    y = x * x
    s = 1.0 / 6227020800.0
    for term in (-1.0 / 39916800.0, 1.0 / 362880.0, -1.0 / 5040.0, 1.0 / 120.0, -1.0 / 6.0, 1.0):
        s = s * y + term
    return -(s * x)


def mode_of(n):
    slot = n >> 4
    device = jnp.where(slot < LAT // 2, slot, LAT + LAT // 2 - 1 - slot)
    order, part = (device << 3) + (n & 7), (n >> 3) & 1
    highest = (order == 0) & (part == 1)
    return jnp.where(highest, NLON // 2, order), jnp.where(highest, 0, part)


def column_of(k):
    return COLS * (k & 31) + (k >> 5)


def halves(x):
    high = x.astype(BF)
    return high, (x - high.astype(F32)).astype(BF)


def fourier_body(sector_ref, kernel_in, fhi_ref, flo_ref, taps_ref, inv_ref, kernel_ref, sem):
    arriving = begin(kernel_in, kernel_ref, sem)
    shape = (16, NLON)
    lane = lanes_of(shape)

    def block(b, unused):
        row = lax.broadcasted_iota(jnp.int32, shape, 0) + 16 * b
        at = pl.ds(pl.multiple_of(16 * b, 16), 16)
        order, part = mode_of(row)
        table = wave(order, part, column_of(lane)) * (2.0 * math.pi / NLON)
        fhi_ref[at, :], flo_ref[at, :] = halves(table)
        return unused

    lax.fori_loop(0, NLON // 16, block, 0)
    shape = (LON, NLON)
    order, part = mode_of(lanes_of(shape))
    column = COLS * lax.broadcasted_iota(jnp.int32, shape, 0)
    weight = jnp.where((order == 0) | (order == NLON // 2), 1.0, 2.0)
    cosine, sine = wave(order, part, column) * weight, wave(order, part + 1, column) * weight
    shape = (16, NLON)
    order, _ = mode_of(lanes_of(shape))
    column = lax.broadcasted_iota(jnp.int32, shape, 0)
    step_cosine, step_sine = wave(order, 0, column), wave(order, 1, column)
    for kap in range(COLS):
        turned = cosine * step_cosine[kap : kap + 1, :] - sine * step_sine[kap : kap + 1, :]
        inv_ref[32 * kap : 32 * kap + 32, :] = turned.astype(BF)
    arriving.wait()
    wide = (kernel_ref.shape[1], 256)
    own = lanes_of(wide) & 31
    channel = lax.broadcasted_iota(jnp.int32, wide, 0)
    picked = (channel == own + sector_ref[0] * CHAN) & (own < CHAN)
    taps_ref[0:9, :] = jnp.dot(
        kernel_ref[...], jnp.where(picked, 1.0, 0.0), precision=lax.Precision.HIGHEST, preferred_element_type=F32
    )


def legendre_body(band_ref, gain_in, p_ref, pt_ref, gain_ref, table, own_ref, square_ref, sem):
    arriving = begin(gain_in, own_ref, sem)
    shape = (8, 128)
    lane = lanes_of(shape)
    order_i = lax.broadcasted_iota(jnp.int32, shape, 0) + band_ref[0] * 8
    order = order_i.astype(F32)
    r = jnp.floor((lane.astype(F32) + 0.5) * (1.0 / LAT))
    slot = lane.astype(F32) - LAT * r
    device = jnp.where(slot < LAT // 2, slot, LAT + LAT // 2 - 1.0 - slot)
    row = jnp.minimum(8.0 * device + r, NLAT - 1.0)
    theta = (row + 0.5) * (math.pi / NLAT)
    cosine, sine = jnp.cos(theta), jnp.sin(theta)
    k = lanes_of((8, 256)).astype(F32) + 1.0
    ratio = jnp.log((2.0 * k - 1.0) / (2.0 * k))
    factor = jnp.sum(jnp.where(k <= order[:, 0:1], ratio, 0.0), axis=1, keepdims=True)
    start = 0.5 * jnp.log((2.0 * order + 1.0) / (4.0 * math.pi)) + 0.5 * factor + order * jnp.log(sine)
    square = order * order
    every = 16

    def block(b, carry):
        before, current, log_scale = carry
        scale = jnp.exp(log_scale)
        for t in range(every):
            degree = b * every + t
            l = degree.astype(F32)
            lower = (l - 1.0) * (l - 1.0)
            alpha = jnp.sqrt((4.0 * l * l - 1.0) / jnp.maximum(l * l - square, 1.0))
            beta = jnp.sqrt(jnp.maximum(lower - square, 0.0) / jnp.maximum(4.0 * lower - 1.0, 1.0))
            fresh = (alpha * cosine) * current - (alpha * beta) * before
            fresh = jnp.where(order_i == degree, 1.0, fresh)
            fresh = jnp.where(order_i > degree, 0.0, fresh)
            before, current = current, fresh
            table[pl.ds(pl.multiple_of(degree * 8, 8), 8), :] = fresh * scale
        largest = jnp.maximum(jnp.abs(before), jnp.abs(current))
        largest = jnp.where(order_i <= b * every + (every - 1), largest, 1.0)
        return before / largest, current / largest, log_scale + jnp.log(largest)

    blank = jnp.zeros(shape, F32)
    lax.fori_loop(0, NLAT // every, block, (blank, blank, start))
    arriving.wait()
    square_ref[0:CHAN, 0:NLAT] = own_ref[...]
    for h in range(2):
        piece = jnp.transpose(square_ref[:, 128 * h : 128 * h + 128])
        piece = jnp.where(lanes_of((128, 128)) < CHAN, piece, 0.0)
        height = 128 if h == 0 else NLAT - 128
        gain_ref[128 * h : 128 * h + height, :] = (piece + turn(piece, 32))[:height, :]
    weight = sine[0:1, :] * (math.pi / NLAT)
    blank = jnp.zeros((128 - NLAT // 2, 128), F32)
    for m in range(8):
        for parity in range(2):
            p = jnp.where(lanes_of((96, 128)) < 96, table[pl.ds(8 * parity + m, 96, stride=16), :], 0.0)
            p_ref[m, 96 * parity : 96 * parity + 96, :] = (p * weight).astype(BF)
            turned = jnp.transpose(jnp.concatenate([p, blank], axis=0))
            pt_ref[m, 96 * parity : 96 * parity + 96, :] = turned[:96, :].astype(BF)


def spectrum_body(recv_ref, fhi_ref, flo_ref, unused_a, unused_b, send_out, full_ref, wide, send_ref, sem):
    wide[...] = recv_ref[...].astype(F32).reshape(LON * 16, 128)
    shape = (LON, 128)
    for e in range(2):
        for h in range(2):
            total = [jnp.zeros(shape, F32)] * PAIRS
            for s in range(4):
                rows = wide[pl.ds(8 * e + 4 * h + s, LON, stride=16), :]
                for q in range(PAIRS):
                    total[q] = jnp.where(inside(shape, 32 * s, CHAN), turn(rows, 32 * s - CHAN * q), total[q])
            for q in range(PAIRS):
                kap = 2 * q + e
                full_ref[32 * kap : 32 * kap + 32, 128 * h : 128 * h + 128] = total[q].astype(BF)
    full = full_ref[...]
    spectrum = jnp.dot(fhi_ref[...], full, preferred_element_type=F32)
    spectrum = spectrum + jnp.dot(flo_ref[...], full, preferred_element_type=F32)
    send_ref[...] = spectrum.astype(BF).reshape(LAT, 16, 256)
    begin(send_ref, send_out, sem).wait()


def row_after(x):
    slot = lax.broadcasted_iota(jnp.int32, x.shape, 0)
    half = LAT // 2
    moved = jnp.where(slot < half - 1, pltpu.roll(x, LAT - 1, 0), pltpu.roll(x, 1, 0))
    return jnp.where(slot == half - 1, swap_halves(x), jnp.where(slot == half, 0.0, moved))


def row_before(x):
    slot = lax.broadcasted_iota(jnp.int32, x.shape, 0)
    half = LAT // 2
    moved = jnp.where(slot < half, pltpu.roll(x, 1, 0), pltpu.roll(x, LAT - 1, 0))
    return jnp.where(slot == LAT - 1, swap_halves(x), jnp.where(slot == 0, 0.0, moved))


def filter_body(
    band_ref, recv_ref, p_ref, pt_ref, gain_ref, taps_ref, send_out, wide, out, send_ref, sem
):
    rows = LAT * 16
    for h in range(2):
        wide[rows * h : rows * h + rows, :] = recv_ref[:, :, 128 * h : 128 * h + 128].astype(F32).reshape(rows, 128)
    shape = (LAT, 128)
    lane = lanes_of(shape)
    blank = jnp.zeros((32, 128), F32)
    order = lax.broadcasted_iota(jnp.int32, (8, 128), 0) + band_ref[0] * 8
    second = ((lanes_of((8, 128)) >> 5) & 1) == 1
    highest = (order == 0) & second
    turn_cosine = jnp.where(highest, -1.0, wave(order, 0, 1)) * (0.5 / math.pi)
    turn_sine = jnp.where(second, -1.0, 1.0) * wave(order, 1, 1) * (0.5 / math.pi)
    used = jnp.where(highest, 0.0, 1.0)
    taps = [taps_ref[i : i + 1, 0:128] for i in range(9)]
    for m in range(8):
        chunks, partners = [], []
        for h in range(2):
            low, high = (wide[pl.ds(rows * h + 8 * p + m, LAT, stride=16), :] for p in range(2))
            for s in range(4):
                chunks.append(jnp.where(lane < 32, turn(low, -32 * s), turn(high, 32 - 32 * s)))
                partners.append(jnp.where(lane < 32, turn(high, -32 * s), turn(low, 32 - 32 * s)))
        mixed = []
        for i in range(3):
            west, here, east = taps[3 * i : 3 * i + 3]
            along = here * (0.5 / math.pi) + (west + east) * turn_cosine[m : m + 1, :]
            across = (east - west) * turn_sine[m : m + 1, :]
            mixed.append([along * chunks[r] + across * partners[r] for r in range(8)])
        above = [row_before(mixed[0][7])] + mixed[0][:7]
        below = mixed[2][1:] + [row_after(mixed[2][0])]
        local = [above[r] + mixed[1][r] + below[r] for r in range(8)]
        if m == 0:
            chunks = [chunk * used[0:1, :] for chunk in chunks]
        mirrored = [swap_halves(chunks[7 - r]) for r in range(4)]
        even = jnp.concatenate([chunks[r] + mirrored[r] for r in range(4)] + [blank], axis=0).astype(BF)
        odd = jnp.concatenate([chunks[r] - mirrored[r] for r in range(4)] + [blank], axis=0).astype(BF)
        halves_back = []
        for parity in range(2):
            at = slice(96 * parity, 96 * parity + 96)
            field = even if (parity + m) % 2 == 0 else odd
            scaled = jnp.dot(p_ref[m, at, :], field, preferred_element_type=F32)
            scaled = scaled * gain_ref[pl.ds(parity, 96, stride=2), :]
            scaled = jnp.concatenate([scaled, blank], axis=0).astype(BF)
            halves_back.append(jnp.dot(pt_ref[m, at, :], scaled, preferred_element_type=F32))
        if m % 2 == 1:
            halves_back.reverse()
        near, far = halves_back[0] + halves_back[1], halves_back[0] - halves_back[1]
        back = [near[LAT * r : LAT * r + LAT, :] for r in range(4)]
        back = back + [swap_halves(far[LAT * r : LAT * r + LAT, :]) for r in (3, 2, 1, 0)]
        back = [back[r] + local[r] for r in range(8)]
        for p in range(2):
            for h in range(2):
                total = jnp.zeros(shape, F32)
                for s in range(4):
                    r = 4 * h + s
                    total = jnp.where(
                        inside(shape, 32 * s, 32), turn(back[r], 32 * s - 32 * p), total
                    )
                out[pl.ds(rows * h + 8 * p + m, LAT, stride=16), :] = total
    for h in range(2):
        send_ref[:, :, 128 * h : 128 * h + 128] = out[rows * h : rows * h + rows, :].astype(BF).reshape(LAT, 16, 128)
    begin(send_ref, send_out, sem).wait()


def synthesis_body(recv_ref, base_ref, inv_ref, send_out, send_ref, out, summed_ref, sem):
    summed_ref[...] = jnp.dot(inv_ref[...], recv_ref[...].reshape(NLON, 256), preferred_element_type=F32)
    summed_ref[...] += base_ref[...].astype(F32)
    shape = (LON, 128)
    for e in range(2):
        for h in range(2):
            for s in range(4):
                total = jnp.zeros(shape, F32)
                for q in range(PAIRS):
                    kap = 2 * q + e
                    rows = summed_ref[32 * kap : 32 * kap + 32, 128 * h : 128 * h + 128]
                    total = jnp.where(inside(shape, CHAN * q, CHAN), turn(rows, CHAN * q - 32 * s), total)
                out[pl.ds(8 * e + 4 * h + s, LON, stride=16), :] = total
    send_ref[...] = out[...].astype(BF).reshape(LON, 16, 128)
    begin(send_ref, send_out, sem).wait()


def mlp_body(recv_ref, gain_ref, win_ref, wout_ref, result_out, summed_ref, out_ref, sems):
    shape = (16, 128)
    lane = lanes_of(shape)
    for tile in range(5):
        for q in range(PAIRS):
            total = jnp.zeros(shape, F32)
            for d in range(128 * tile // CHAN, (128 * tile + 127) // CHAN + 1):
                off = CHAN * d - 128 * tile
                piece = turn(recv_ref[d].astype(F32), off - CHAN * q)
                total = jnp.where((lane >= off) & (lane < off + CHAN), piece, total)
            summed_ref[16 * q : 16 * q + 16, 128 * tile : 128 * tile + 128] = total
    summed = summed_ref[...]
    mean = jnp.sum(summed * summed, axis=1, keepdims=True) * (1.0 / summed.shape[1])
    normed = (summed * lax.rsqrt(mean + EPS) * gain_ref[...]).astype(BF)
    hidden = jnp.dot(normed, win_ref[...], preferred_element_type=F32)
    hidden = (0.5 * hidden * (1.0 + lax.erf(hidden * math.sqrt(0.5)))).astype(BF)
    copies = []
    for i, (start, width) in enumerate(((0, 384), (384, 256))):
        at = slice(start, start + width)
        result = summed_ref[:, at] + jnp.dot(hidden, wout_ref[:, at], preferred_element_type=F32)
        out_ref[:, at] = result.astype(BF)
        at = pl.ds(start, width)
        copies.append(begin(out_ref.at[:, at], result_out.at[:, at], sems.at[i]))
    for copy in copies:
        copy.wait()


def on_device(latent_field, spectral_filter, conv_weight, norm_gain, weight_in, weight_out):
    channels = latent_field.shape[0]
    points = COLS * ROWS
    table, circle, group, mode = (NLON, NLON), (NLON, 256), (LON, 16, 128), (LAT, 16, 256)
    field = jnp.transpose(latent_field, (2, 1, 0)).reshape(points, channels)
    pieces = call(
        pack_body,
        [(group, BF, HBM)],
        [(field, HBM)],
        [VMEM((points, channels), BF), VMEM(group, BF), pltpu.SemaphoreType.DMA((5,))],
        name="pack",
    )
    pieces = lax.all_to_all(pieces, "lon", 0, 0, tiled=True)

    sector = lax.axis_index("lon").astype(jnp.int32).reshape(1)
    band = lax.axis_index("lat").astype(jnp.int32).reshape(1)
    fhi, flo, taps, inverse = call(
        fourier_body,
        [(table, BF, VMEM), (table, BF, VMEM), ((16, 256), F32, VMEM), (table, BF, VMEM)],
        [(sector, SMEM), (conv_weight, HBM)],
        [VMEM(conv_weight.shape, F32), pltpu.SemaphoreType.DMA],
        name="fourier_tables",
        flops=10_000_000,
    )
    polynomials = (8, NLAT, 128)
    p, pt, gain = call(
        legendre_body,
        [(polynomials, BF, VMEM), (polynomials, BF, VMEM), ((NLAT, 128), F32, VMEM)],
        [(band, SMEM), (spectral_filter, HBM)],
        [VMEM((NLAT * 8, 128), F32), VMEM((CHAN, NLAT), F32), VMEM((128, 256), F32), pltpu.SemaphoreType.DMA],
        name="legendre_tables",
        flops=10_000_000,
    )
    norm_gain = norm_gain.reshape(1, channels)
    modes, full = call(
        spectrum_body,
        [(mode, BF, HBM), (circle, BF, VMEM)],
        [(pieces, VMEM), (fhi, VMEM), (flo, VMEM), (gain, VMEM), (norm_gain, HBM)],
        [VMEM((LON * 16, 128), F32), VMEM(mode, BF), pltpu.SemaphoreType.DMA],
        name="spectrum",
    )
    modes = lax.all_to_all(modes, "lat", 0, 0, tiled=True, axis_index_groups=[SLOTS])
    modes = call(
        filter_body,
        [(mode, BF, HBM)],
        [(band, SMEM), (modes, VMEM), (p, VMEM), (pt, VMEM), (gain, VMEM), (taps, VMEM)],
        [VMEM((2 * LAT * 16, 128), F32)] * 2 + [VMEM(mode, BF), pltpu.SemaphoreType.DMA],
        name="filter",
    )
    modes = lax.all_to_all(modes, "lat", 0, 0, tiled=True, axis_index_groups=[SLOTS])
    pieces = call(
        synthesis_body,
        [(group, BF, HBM)],
        [(modes, VMEM), (full, VMEM), (inverse, VMEM)],
        [VMEM(group, BF), VMEM((LON * 16, 128), F32), VMEM(circle, F32), pltpu.SemaphoreType.DMA],
        name="synthesis",
    )
    pieces = lax.all_to_all(pieces, "lon", 0, 0, tiled=True)
    result = call(
        mlp_body,
        [((points, channels), BF, HBM)],
        [(pieces, VMEM), (norm_gain, VMEM), (weight_in, VMEM), (weight_out, VMEM)],
        [VMEM((points, channels), F32), VMEM((points, channels), BF), pltpu.SemaphoreType.DMA((2,))],
        name="mlp",
    )
    return jnp.transpose(result.reshape(COLS, ROWS, channels), (2, 1, 0))


def solution(mesh):
    in_specs = (P(None, "lat", "lon"), P("lon", None), P(), P(), P(), P())
    return jax.shard_map(on_device, mesh=mesh, in_specs=in_specs, out_specs=P(None, "lat", "lon"), check_vma=False)
```
